32 devices in a mesh: groups: 2 (over y), space: 4 (over z), dp: 4 (over x, core).
Axes of the slice: x: 2, y: 2, z: 4, core: 2. Of those that a mesh axis runs over, the one named last changes fastest.
Arguments:
- grad_mid: bfloat16 [8, 8, 180, 768], P(('groups', 'dp'), 'space'), parts along dimension 0, may hold values from -6 to 6
- spectrum: bfloat16 [2, 8, 8, 64, 768], P(None, ('groups', 'dp'), None, 'space'), parts along dimension 1, may hold values from -6 to 6
- filter_inner: bfloat16 [2, 8, 96, 96], replicated, may hold values from -0.4375 to 0.4375
- filter_outer: bfloat16 [2, 8, 96, 96], replicated, may hold values from -0.4375 to 0.4375
- cutoff: int32 [64], replicated, may hold values from 1 to 4, as said below
- normed_mid: bfloat16 [8, 8, 180, 768], P(('groups', 'dp'), 'space'), parts along dimension 0, may hold values from -6 to 6
- hidden_grad: bfloat16 [8, 8, 180, 3072], P(('groups', 'dp'), 'space'), parts along dimension 0, may hold values from -6 to 6
- power_start: bfloat16 [3072, 32], replicated, may hold values from -5 to 5
Outputs:
- grad_input: bfloat16 [8, 8, 180, 768], P(('groups', 'dp'), 'space'), parts along dimension 0
- grad_inner: float32 [4, 8, 96, 96], P('groups', 'dp'), parts along dimension 0
- grad_outer: float32 [4, 8, 96, 96], P('groups', 'dp'), parts along dimension 0
- left_factor: float32 [1536, 32], P('groups'), parts along dimension 0
- right_factor: float32 [6144, 32], P(('groups', 'space', 'dp')), parts along dimension 0
The draws below stay inside these ranges and needn't reach their ends.
There are 2 independent parts, one for each index of `groups`. The reference program is written for one: setup_inputs(seed, part) draws one part's arguments, and reference() takes and returns one part's arrays. A program takes and returns all parts, laid end to end along the dimension named above; an argument that names none is the same for every part. Nothing has to cross between parts.
Inputs may be any that keep to these rules, and one draw needn't show every extreme that they name: A latitude frequency f of longitude mode k is retained where |f| < cutoff[k]; some mode has 4 and some has 1.
All inputs are finite; a program needn't handle non-finite values.
Results may differ from the reference program's by a relative error of at most 0.015.
Values may be sent and summed in bfloat16 or wider, within the bound.
A program may use at most 64 MiB of HBM per device.

```python
import math
import jax
import jax.numpy as jnp
from jax import lax

D = 768
NB = 8
BS = 96
FF = 3072
LON = 180
KLON = 64
RANK = 32
SAMPLES = 4
LAT = 8


def draw_cutoff(key, part):
    key = jax.random.fold_in(key, 11)
    value_key, order_key = jax.random.split(key)
    values = jax.random.randint(value_key, (KLON,), 1, LAT // 2 + 1, dtype=jnp.int32)
    order = jax.random.permutation(order_key, KLON)
    values = values.at[order[0]].set(LAT // 2)
    values = values.at[order[1]].set(1)
    return values.astype(jnp.int32)


def strengthened(array, stream_key, source, target, parts, factor):
    owner, partner = [(jnp.arange(array.shape[position]) // (array.shape[position] // parts)).reshape([-1 if axis == position else 1 for axis in range(array.ndim)]) for position in (source, target)]
    chosen = jax.random.permutation(stream_key, parts)[partner]
    strong = (owner == chosen) | (owner == (partner + parts // 2) % parts)
    return jnp.where(strong, factor * array, array)


def block_levels(own_key, shape, pieces, low, high):
    def one(dim, blocks):
        heights = jax.random.uniform(jax.random.fold_in(jax.random.fold_in(own_key, 6), dim), (blocks,), jnp.float32, low / len(pieces), high / len(pieces))
        return jnp.repeat(jnp.exp(heights), shape[dim] // blocks).reshape((-1,) + (1,) * (len(shape) - dim - 1))

    level = one(*pieces[0])
    for cut in pieces[1:]:
        level = level * one(*cut)
    return level


def centred(key, extent, width, limit, cuts=(), kind=jnp.bfloat16):
    gain = block_levels(key, extent, cuts, -0.22, 0.18) if cuts else 1.0
    result = jax.random.normal(key, extent, jnp.float32) * width * gain
    return jnp.minimum(jnp.maximum(result, -limit), limit).astype(kind)


def bell_draw_with(rng, extent, width, reach, cuts, heavy, held_as=jnp.bfloat16):
    array = width * jax.random.normal(rng, extent, jnp.float32)
    if cuts:
        array = array * block_levels(rng, extent, cuts, -0.22, 0.18)
    return jnp.clip(strengthened(array, jax.random.fold_in(rng, 3), *heavy), -reach, reach).astype(held_as)


def setup_inputs(seed: int = 0, part: int = 0) -> dict:
    arg_keys = jax.random.split(jax.random.key(seed), 9)
    own_keys = jax.random.split(jax.random.fold_in(arg_keys[8], part), 9)
    grad_mid = centred(own_keys[0], (SAMPLES, LAT, LON, D), 1.0, 6.0, ((0, 4), (1, 4)))
    spectrum = centred(own_keys[1], (2, SAMPLES, LAT, KLON, D), 1.0, 6.0, ((1, 4), (3, 4)))
    filter_inner = centred(arg_keys[2], (2, NB, BS, BS), (2 * BS) ** -0.5, 0.4375)
    filter_outer = centred(arg_keys[3], (2, NB, BS, BS), (2 * BS) ** -0.5, 0.4375)
    cutoff = draw_cutoff(jax.random.fold_in(arg_keys[8], 71), part)
    normed_mid = centred(own_keys[5], (SAMPLES, LAT, LON, D), 1.0, 6.0, ((0, 4), (1, 4)))
    hidden_grad = bell_draw_with(own_keys[6], (SAMPLES, LAT, LON, FF), 1.0, 6.0, ((0, 4), (1, 4)), (1, 3, 4, 2.0))
    power_start = centred(arg_keys[7], (FF, RANK), 1.0, 5.0)
    return dict(grad_mid=grad_mid, spectrum=spectrum, filter_inner=filter_inner, filter_outer=filter_outer, cutoff=cutoff, normed_mid=normed_mid, hidden_grad=hidden_grad, power_start=power_start)


HIGHEST = lax.Precision.HIGHEST

def angle_table(left_count, right_count, length):
    left_index = jnp.arange(left_count, dtype=jnp.int32)[:, None]
    right_index = jnp.arange(right_count, dtype=jnp.int32)[None, :]
    angles = (left_index * right_index % length).astype(jnp.float32) * (2.0 * math.pi / length)
    return (jnp.cos(angles), jnp.sin(angles))

def lon_forward(grid_values, cosine_table, sine_table, factor):
    real_part = jnp.einsum('srlc,kl->srkc', grid_values, cosine_table, precision=HIGHEST) * factor
    imag_part = -jnp.einsum('srlc,kl->srkc', grid_values, sine_table, precision=HIGHEST) * factor
    return jnp.stack([real_part, imag_part])

def lat_forward(complex_pair, cosine_table, sine_table):
    real_part = jnp.einsum('jt,stkc->sjkc', cosine_table, complex_pair[0], precision=HIGHEST) + jnp.einsum('jt,stkc->sjkc', sine_table, complex_pair[1], precision=HIGHEST)
    imag_part = jnp.einsum('jt,stkc->sjkc', cosine_table, complex_pair[1], precision=HIGHEST) - jnp.einsum('jt,stkc->sjkc', sine_table, complex_pair[0], precision=HIGHEST)
    return jnp.stack([real_part, imag_part])

def lat_adjoint(complex_pair, cosine_table, sine_table):
    real_part = jnp.einsum('jt,sjkc->stkc', cosine_table, complex_pair[0], precision=HIGHEST) - jnp.einsum('jt,sjkc->stkc', sine_table, complex_pair[1], precision=HIGHEST)
    imag_part = jnp.einsum('jt,sjkc->stkc', sine_table, complex_pair[0], precision=HIGHEST) + jnp.einsum('jt,sjkc->stkc', cosine_table, complex_pair[1], precision=HIGHEST)
    return jnp.stack([real_part, imag_part])

def lon_adjoint(complex_pair, cosine_table, sine_table, factor):
    summed = jnp.einsum('srkc,kl->srlc', complex_pair[0], cosine_table, precision=HIGHEST) - jnp.einsum('srkc,kl->srlc', complex_pair[1], sine_table, precision=HIGHEST)
    return summed * factor

def mode_weight(lat_count, first_mode, mode_count, cut_local):
    frequency = jnp.arange(lat_count, dtype=jnp.int32)
    signed = jnp.where(frequency < lat_count // 2, frequency, frequency - lat_count)
    mode_index = first_mode + jnp.arange(mode_count, dtype=jnp.int32)
    double = jnp.where(mode_index == 0, 1.0, 2.0)
    retained = jnp.abs(signed)[:, None] < cut_local[None, :]
    return jnp.where(retained, double[None, :], 0.0).astype(jnp.float32)

def complex_product(real_part, imag_part, weights):
    out_real = jnp.einsum('rbi,bio->rbo', real_part, weights[0], precision=HIGHEST) - jnp.einsum('rbi,bio->rbo', imag_part, weights[1], precision=HIGHEST)
    out_imag = jnp.einsum('rbi,bio->rbo', real_part, weights[1], precision=HIGHEST) + jnp.einsum('rbi,bio->rbo', imag_part, weights[0], precision=HIGHEST)
    return (out_real, out_imag)

def spectral_filter(real_part, imag_part, inner_weights, outer_weights):
    hidden_real, hidden_imag = complex_product(real_part, imag_part, inner_weights)
    return complex_product(jax.nn.gelu(hidden_real, approximate=False), jax.nn.gelu(hidden_imag, approximate=False), outer_weights)

def filter_backward(spectrum_pair, cotangent, inner_weights, outer_weights):

    def shaped(values):
        return values.reshape(-1, NB, BS)
    outputs, pullback = jax.vjp(spectral_filter, shaped(spectrum_pair[0]), shaped(spectrum_pair[1]), inner_weights, outer_weights)
    gradients = pullback((shaped(cotangent[0]), shaped(cotangent[1])))
    block_shape = spectrum_pair.shape[1:]
    mode_grad = jnp.stack([gradients[0].reshape(block_shape), gradients[1].reshape(block_shape)])
    return (mode_grad, gradients[2], gradients[3])

def orthonormal(sketch):
    gram_matrix = jnp.dot(sketch.T, sketch, precision=HIGHEST)
    cholesky_factor = jnp.linalg.cholesky(gram_matrix)
    return lax.linalg.triangular_solve(cholesky_factor, sketch, left_side=False, lower=True, transpose_a=True)

def reference(grad_mid, spectrum, filter_inner, filter_outer, cutoff, normed_mid, hidden_grad, power_start):
    factor = 1.0 / math.sqrt(LAT * LON)
    grad_float = grad_mid.astype(jnp.float32)
    lon_cos, lon_sin = angle_table(KLON, LON, LON)
    lat_cos, lat_sin = angle_table(LAT, LAT, LAT)
    mode_values = lat_forward(lon_forward(grad_float, lon_cos, lon_sin, factor), lat_cos, lat_sin)
    weight = mode_weight(LAT, 0, KLON, cutoff)
    cotangent = mode_values * weight[None, None, :, :, None]
    mode_grad, inner_grad, outer_grad = filter_backward(spectrum.astype(jnp.float32), cotangent, filter_inner.astype(jnp.float32), filter_outer.astype(jnp.float32))
    spectral_grad = lon_adjoint(lat_adjoint(mode_grad, lat_cos, lat_sin), lon_cos, lon_sin, factor)
    grad_input = (grad_float + spectral_grad).astype(jnp.bfloat16)
    grad_factor = 1.0 / math.sqrt(SAMPLES * LAT * KLON)
    tokens_mid = normed_mid.reshape(-1, D)
    tokens_grad = hidden_grad.reshape(-1, FF)
    probe = jnp.dot(tokens_grad.astype(jnp.float32), power_start.astype(jnp.float32), preferred_element_type=jnp.float32).astype(jnp.bfloat16)
    sketch = jnp.dot(tokens_mid.T.astype(jnp.float32), probe.astype(jnp.float32), preferred_element_type=jnp.float32)
    left_factor = orthonormal(sketch)
    left_round = left_factor.astype(jnp.bfloat16)
    mixed = jnp.dot(tokens_mid.astype(jnp.float32), left_round.astype(jnp.float32), preferred_element_type=jnp.float32).astype(jnp.bfloat16)
    right_factor = jnp.dot(tokens_grad.T.astype(jnp.float32), mixed.astype(jnp.float32), preferred_element_type=jnp.float32) * (1.0 / math.sqrt(SAMPLES * LAT * LON))
    return (grad_input, inner_grad * grad_factor, outer_grad * grad_factor, left_factor, right_factor)
```

```python
import math

import jax
import jax.numpy as jnp
from jax import lax
from jax.sharding import PartitionSpec as P

D = 768
NB = 8
BS = 96
FF = 3072
LON = 180
KLON = 64


HIGHEST = lax.Precision.HIGHEST


def angle_table(left_count, right_count, length):
    left_index = jnp.arange(left_count, dtype=jnp.int32)[:, None]
    right_index = jnp.arange(right_count, dtype=jnp.int32)[None, :]
    angles = (left_index * right_index % length).astype(jnp.float32) * (2.0 * math.pi / length)
    return (jnp.cos(angles), jnp.sin(angles))


def lon_forward(grid_values, cosine_table, sine_table, factor):
    real_part = jnp.einsum("srlc,kl->srkc", grid_values, cosine_table) * factor
    imag_part = -jnp.einsum("srlc,kl->srkc", grid_values, sine_table) * factor
    return jnp.stack([real_part, imag_part])


def lat_forward(complex_pair, cosine_table, sine_table):
    real_part = jnp.einsum(
        "jt,stkc->sjkc", cosine_table, complex_pair[0]
    ) + jnp.einsum("jt,stkc->sjkc", sine_table, complex_pair[1])
    imag_part = jnp.einsum(
        "jt,stkc->sjkc", cosine_table, complex_pair[1]
    ) - jnp.einsum("jt,stkc->sjkc", sine_table, complex_pair[0])
    return jnp.stack([real_part, imag_part])


def lat_adjoint(complex_pair, cosine_table, sine_table):
    real_part = jnp.einsum(
        "jt,sjkc->stkc", cosine_table, complex_pair[0]
    ) - jnp.einsum("jt,sjkc->stkc", sine_table, complex_pair[1])
    imag_part = jnp.einsum(
        "jt,sjkc->stkc", sine_table, complex_pair[0]
    ) + jnp.einsum("jt,sjkc->stkc", cosine_table, complex_pair[1])
    return jnp.stack([real_part, imag_part])


def lon_adjoint(complex_pair, cosine_table, sine_table, factor):
    summed = jnp.einsum(
        "srkc,kl->srlc", complex_pair[0], cosine_table
    ) - jnp.einsum("srkc,kl->srlc", complex_pair[1], sine_table)
    return summed * factor


def mode_weight(lat_count, first_mode, mode_count, cut_local):
    frequency = jnp.arange(lat_count, dtype=jnp.int32)
    signed = jnp.where(frequency < lat_count // 2, frequency, frequency - lat_count)
    mode_index = first_mode + jnp.arange(mode_count, dtype=jnp.int32)
    double = jnp.where(mode_index == 0, 1.0, 2.0)
    retained = jnp.abs(signed)[:, None] < cut_local[None, :]
    return jnp.where(retained, double[None, :], 0.0).astype(jnp.float32)


def complex_product(real_part, imag_part, weights):
    out_real = jnp.einsum("rbi,bio->rbo", real_part, weights[0]) - jnp.einsum(
        "rbi,bio->rbo", imag_part, weights[1]
    )
    out_imag = jnp.einsum("rbi,bio->rbo", real_part, weights[1]) + jnp.einsum(
        "rbi,bio->rbo", imag_part, weights[0]
    )
    return (out_real, out_imag)


def spectral_filter(real_part, imag_part, inner_weights, outer_weights):
    hidden_real, hidden_imag = complex_product(real_part, imag_part, inner_weights)
    return complex_product(
        jax.nn.gelu(hidden_real, approximate=False),
        jax.nn.gelu(hidden_imag, approximate=False),
        outer_weights,
    )


def filter_backward(spectrum_pair, cotangent, inner_weights, outer_weights):

    def shaped(values):
        return values.reshape(-1, NB, BS)

    outputs, pullback = jax.vjp(
        spectral_filter,
        shaped(spectrum_pair[0]),
        shaped(spectrum_pair[1]),
        inner_weights,
        outer_weights,
    )
    gradients = pullback((shaped(cotangent[0]), shaped(cotangent[1])))
    block_shape = spectrum_pair.shape[1:]
    mode_grad = jnp.stack([gradients[0].reshape(block_shape), gradients[1].reshape(block_shape)])
    return (mode_grad, gradients[2], gradients[3])


def orthonormal(sketch):
    gram_matrix = jnp.dot(sketch.T, sketch, precision=HIGHEST)
    cholesky_factor = jnp.linalg.cholesky(gram_matrix)
    return lax.linalg.triangular_solve(
        cholesky_factor, sketch, left_side=False, lower=True, transpose_a=True
    )


def body(
    grad_mid, spectrum, filter_inner, filter_outer, cutoff, normed_mid, hidden_grad, power_start
):
    space_count = lax.axis_size("space")
    data_count = lax.axis_size("dp")
    sample_count = grad_mid.shape[0]
    lat_count = grad_mid.shape[1] * space_count
    mode_local = KLON // space_count
    factor = 1.0 / math.sqrt(lat_count * LON)
    tokens_mid = normed_mid.reshape(-1, D)
    tokens_grad = hidden_grad.reshape(-1, FF)
    probe = jnp.dot(tokens_grad, power_start, preferred_element_type=jnp.float32).astype(
        jnp.bfloat16
    )
    sketch_local = jnp.dot(tokens_mid.T, probe, preferred_element_type=jnp.float32)
    sketch = lax.psum(sketch_local, ("space", "dp"))
    grad_float = grad_mid.astype(jnp.float32)
    lon_cos, lon_sin = angle_table(KLON, LON, LON)
    lat_cos, lat_sin = angle_table(lat_count, lat_count, lat_count)
    row_spectra = lon_forward(grad_float, lon_cos, lon_sin, factor)
    mode_values = lat_forward(
        lax.all_to_all(
            row_spectra.astype(jnp.bfloat16), "space", split_axis=3, concat_axis=2, tiled=True
        ).astype(jnp.float32),
        lat_cos,
        lat_sin,
    )
    first_mode = lax.axis_index("space") * mode_local
    cut_local = lax.dynamic_slice_in_dim(cutoff, first_mode, mode_local)
    weight = mode_weight(lat_count, first_mode, mode_local, cut_local)
    cotangent = mode_values * weight[None, None, :, :, None]
    mode_grad, inner_grad, outer_grad = filter_backward(
        spectrum.astype(jnp.float32),
        cotangent,
        filter_inner.astype(jnp.float32),
        filter_outer.astype(jnp.float32),
    )
    back = lat_adjoint(mode_grad, lat_cos, lat_sin)
    row_back = lax.all_to_all(
        back.astype(jnp.bfloat16), "space", split_axis=2, concat_axis=3, tiled=True
    ).astype(jnp.float32)
    spectral_grad = lon_adjoint(row_back, lon_cos, lon_sin, factor)
    grad_input = (grad_float + spectral_grad).astype(jnp.bfloat16)
    inner_grad, outer_grad = (
        lax.psum_scatter(
            inner_grad.astype(jnp.bfloat16), "dp", scatter_dimension=1, tiled=True
        ).astype(jnp.float32),
        lax.psum_scatter(
            outer_grad.astype(jnp.bfloat16), "dp", scatter_dimension=1, tiled=True
        ).astype(jnp.float32),
    )
    inner_grad, outer_grad = (
        lax.psum(inner_grad.astype(jnp.bfloat16), "space").astype(jnp.float32),
        lax.psum(outer_grad.astype(jnp.bfloat16), "space").astype(jnp.float32),
    )
    grad_factor = 1.0 / math.sqrt(sample_count * data_count * lat_count * KLON)
    left_factor = orthonormal(sketch)
    left_round = left_factor.astype(jnp.bfloat16)
    mixed = jnp.dot(tokens_mid, left_round, preferred_element_type=jnp.float32).astype(jnp.bfloat16)
    right_sum = lax.psum_scatter(
        jnp.dot(tokens_grad.T, mixed, preferred_element_type=jnp.float32),
        ("space", "dp"),
        scatter_dimension=0,
        tiled=True,
    )
    right_factor = right_sum * (1.0 / math.sqrt(sample_count * data_count * lat_count * LON))
    return (
        grad_input,
        inner_grad * grad_factor,
        outer_grad * grad_factor,
        left_factor,
        right_factor,
    )


def solution(mesh):
    in_specs = (
        P(("groups", "dp"), "space", None, None),
        P(None, ("groups", "dp"), None, "space", None),
        P(),
        P(),
        P(),
        P(("groups", "dp"), "space", None, None),
        P(("groups", "dp"), "space", None, None),
        P(),
    )
    out_specs = (
        P(("groups", "dp"), "space", None, None),
        P("groups", "dp", None, None),
        P("groups", "dp", None, None),
        P("groups", None),
        P(("groups", "space", "dp"), None),
    )
    return jax.shard_map(body, mesh=mesh, in_specs=in_specs, out_specs=out_specs, check_vma=False)
```

```python
import math

import jax
import jax.numpy as jnp
import numpy as np
from jax import lax
from jax.experimental import pallas as pl
from jax.experimental.pallas import tpu as pltpu
from jax.sharding import PartitionSpec as P

D = 768
NB = 8
BS = 96
FF = 3072
LON = 180
KLON = 64


HIGHEST = lax.Precision.HIGHEST


def angle_table(left_count, right_count, length):
    left_index = jnp.arange(left_count, dtype=jnp.int32)[:, None]
    right_index = jnp.arange(right_count, dtype=jnp.int32)[None, :]
    angles = (left_index * right_index % length).astype(jnp.float32) * (2.0 * math.pi / length)
    return (jnp.cos(angles), jnp.sin(angles))


def lon_forward(grid_values, cosine_table, sine_table, factor):
    real_part = jnp.einsum("srlc,kl->srkc", grid_values, cosine_table) * factor
    imag_part = -jnp.einsum("srlc,kl->srkc", grid_values, sine_table) * factor
    return jnp.stack([real_part, imag_part])


def lat_forward(complex_pair, cosine_table, sine_table):
    real_part = jnp.einsum(
        "jt,stkc->sjkc", cosine_table, complex_pair[0]
    ) + jnp.einsum("jt,stkc->sjkc", sine_table, complex_pair[1])
    imag_part = jnp.einsum(
        "jt,stkc->sjkc", cosine_table, complex_pair[1]
    ) - jnp.einsum("jt,stkc->sjkc", sine_table, complex_pair[0])
    return jnp.stack([real_part, imag_part])


def lat_adjoint(complex_pair, cosine_table, sine_table):
    real_part = jnp.einsum(
        "jt,sjkc->stkc", cosine_table, complex_pair[0]
    ) - jnp.einsum("jt,sjkc->stkc", sine_table, complex_pair[1])
    imag_part = jnp.einsum(
        "jt,sjkc->stkc", sine_table, complex_pair[0]
    ) + jnp.einsum("jt,sjkc->stkc", cosine_table, complex_pair[1])
    return jnp.stack([real_part, imag_part])


def lon_adjoint(complex_pair, cosine_table, sine_table, factor):
    summed = jnp.einsum(
        "srkc,kl->srlc", complex_pair[0], cosine_table
    ) - jnp.einsum("srkc,kl->srlc", complex_pair[1], sine_table)
    return summed * factor


def mode_weight(lat_count, first_mode, mode_count, cut_local):
    frequency = jnp.arange(lat_count, dtype=jnp.int32)
    signed = jnp.where(frequency < lat_count // 2, frequency, frequency - lat_count)
    mode_index = first_mode + jnp.arange(mode_count, dtype=jnp.int32)
    double = jnp.where(mode_index == 0, 1.0, 2.0)
    retained = jnp.abs(signed)[:, None] < cut_local[None, :]
    return jnp.where(retained, double[None, :], 0.0).astype(jnp.float32)


def complex_product(real_part, imag_part, weights):
    out_real = jnp.einsum("rbi,bio->rbo", real_part, weights[0]) - jnp.einsum(
        "rbi,bio->rbo", imag_part, weights[1]
    )
    out_imag = jnp.einsum("rbi,bio->rbo", real_part, weights[1]) + jnp.einsum(
        "rbi,bio->rbo", imag_part, weights[0]
    )
    return (out_real, out_imag)


def spectral_filter(real_part, imag_part, inner_weights, outer_weights):
    hidden_real, hidden_imag = complex_product(real_part, imag_part, inner_weights)
    return complex_product(
        jax.nn.gelu(hidden_real, approximate=False),
        jax.nn.gelu(hidden_imag, approximate=False),
        outer_weights,
    )


def filter_backward(spectrum_pair, cotangent, inner_weights, outer_weights):

    def shaped(values):
        return values.reshape(-1, NB, BS)

    outputs, pullback = jax.vjp(
        spectral_filter,
        shaped(spectrum_pair[0]),
        shaped(spectrum_pair[1]),
        inner_weights,
        outer_weights,
    )
    gradients = pullback((shaped(cotangent[0]), shaped(cotangent[1])))
    block_shape = spectrum_pair.shape[1:]
    mode_grad = jnp.stack([gradients[0].reshape(block_shape), gradients[1].reshape(block_shape)])
    return (mode_grad, gradients[2], gradients[3])


def orthonormal(sketch):
    gram_matrix = jnp.dot(sketch.T, sketch, precision=HIGHEST)
    cholesky_factor = jnp.linalg.cholesky(gram_matrix)
    return lax.linalg.triangular_solve(
        cholesky_factor, sketch, left_side=False, lower=True, transpose_a=True
    )


def body(
    grad_mid, spectrum, filter_inner, filter_outer, cutoff, normed_mid, hidden_grad, power_start
):
    space_count = lax.axis_size("space")
    data_count = lax.axis_size("dp")
    sample_count = grad_mid.shape[0]
    lat_count = grad_mid.shape[1] * space_count
    mode_local = KLON // space_count
    factor = 1.0 / math.sqrt(lat_count * LON)
    tokens_mid = normed_mid.reshape(-1, D)
    tokens_grad = hidden_grad.reshape(-1, FF)
    probe = jnp.dot(tokens_grad, power_start, preferred_element_type=jnp.float32).astype(
        jnp.bfloat16
    )
    sketch_local = jnp.dot(tokens_mid.T, probe, preferred_element_type=jnp.float32)
    sketch = lax.psum(sketch_local, ("space", "dp"))
    grad_float = grad_mid.astype(jnp.float32)
    lon_cos, lon_sin = angle_table(KLON, LON, LON)
    lat_cos, lat_sin = angle_table(lat_count, lat_count, lat_count)
    row_spectra = lon_forward(grad_float, lon_cos, lon_sin, factor)
    mode_values = lat_forward(
        lax.all_to_all(
            row_spectra.astype(jnp.bfloat16), "space", split_axis=3, concat_axis=2, tiled=True
        ).astype(jnp.float32),
        lat_cos,
        lat_sin,
    )
    first_mode = lax.axis_index("space") * mode_local
    cut_local = lax.dynamic_slice_in_dim(cutoff, first_mode, mode_local)
    weight = mode_weight(lat_count, first_mode, mode_local, cut_local)
    cotangent = mode_values * weight[None, None, :, :, None]
    mode_grad, inner_grad, outer_grad = filter_backward(
        spectrum.astype(jnp.float32),
        cotangent,
        filter_inner.astype(jnp.float32),
        filter_outer.astype(jnp.float32),
    )
    back = lat_adjoint(mode_grad, lat_cos, lat_sin)
    row_back = lax.all_to_all(
        back.astype(jnp.bfloat16), "space", split_axis=2, concat_axis=3, tiled=True
    ).astype(jnp.float32)
    spectral_grad = lon_adjoint(row_back, lon_cos, lon_sin, factor)
    grad_input = (grad_float + spectral_grad).astype(jnp.bfloat16)
    inner_grad, outer_grad = (
        lax.psum_scatter(
            inner_grad.astype(jnp.bfloat16), "dp", scatter_dimension=1, tiled=True
        ).astype(jnp.float32),
        lax.psum_scatter(
            outer_grad.astype(jnp.bfloat16), "dp", scatter_dimension=1, tiled=True
        ).astype(jnp.float32),
    )
    inner_grad, outer_grad = (
        lax.psum(inner_grad.astype(jnp.bfloat16), "space").astype(jnp.float32),
        lax.psum(outer_grad.astype(jnp.bfloat16), "space").astype(jnp.float32),
    )
    grad_factor = 1.0 / math.sqrt(sample_count * data_count * lat_count * KLON)
    left_factor = orthonormal(sketch)
    left_round = left_factor.astype(jnp.bfloat16)
    mixed = jnp.dot(tokens_mid, left_round, preferred_element_type=jnp.float32).astype(jnp.bfloat16)
    right_sum = lax.psum_scatter(
        jnp.dot(tokens_grad.T, mixed, preferred_element_type=jnp.float32),
        ("space", "dp"),
        scatter_dimension=0,
        tiled=True,
    )
    right_factor = right_sum * (1.0 / math.sqrt(sample_count * data_count * lat_count * LON))
    return (
        grad_input,
        inner_grad * grad_factor,
        outer_grad * grad_factor,
        left_factor,
        right_factor,
    )


def fused_tables(space_count, row_count):
    lat_count = space_count * row_count
    mode_local = KLON // space_count
    factor = 1.0 / math.sqrt(lat_count * LON)
    angle = (np.outer(np.arange(KLON), np.arange(LON)) % LON) * (2.0 * math.pi / LON)
    pair = np.stack([np.cos(angle), -np.sin(angle)]) * factor
    lon_table = (
        pair.reshape(2, space_count, mode_local, LON)
        .transpose(1, 0, 2, 3)
        .reshape(2 * KLON, LON)
    )
    spread = np.zeros((row_count, LON, space_count, row_count, 2 * mode_local))
    for row in range(row_count):
        spread[row, :, :, row, :] = lon_table.T.reshape(LON, space_count, 2 * mode_local)
    spread = spread.reshape(row_count, LON, space_count * row_count * 2 * mode_local)
    angle = (np.outer(np.arange(lat_count), np.arange(lat_count)) % lat_count) * (
        2.0 * math.pi / lat_count
    )
    cosine, sine = np.cos(angle), np.sin(angle)
    mix = np.stack([np.stack([cosine, sine], -1), np.stack([-sine, cosine], -1)])
    lat_table = np.einsum("ojti,kl->ojktil", mix, np.eye(mode_local)).reshape(
        2 * lat_count * mode_local, 2 * lat_count * mode_local
    )
    as_bf16 = lambda values: jnp.asarray(values.astype(np.float32), jnp.bfloat16)
    return as_bf16(lon_table), as_bf16(spread), as_bf16(lat_table), as_bf16(lat_table.T.copy())


NN = (((1,), (0,)), ((), ()))
NT = (((1,), (1,)), ((), ()))
TN = (((0,), (0,)), ((), ()))


def mxu(left, right, dims=NN):
    return lax.dot_general(left, right, dims, preferred_element_type=jnp.float32)


def fused_kernel(
    grid_hbm,
    spectrum_hbm,
    inner_hbm,
    outer_hbm,
    cutoff_ref,
    normed_hbm,
    hidden_hbm,
    start_hbm,
    lon_ref,
    spread_ref,
    lat_ref,
    back_ref,
    grid_out,
    weight_out,
    left_out,
    right_out,
    grid_ref,
    spectrum_ref,
    inner_ref,
    outer_ref,
    normed_ref,
    hidden_ref,
    start_ref,
    inner_wide,
    outer_wide,
    act_ref,
    slope_ref,
    cot_ref,
    hid_ref,
    xg_ref,
    mode_send,
    mode_recv,
    back_send,
    back_recv,
    sketch_local,
    sketch_recv,
    sketch_part,
    sketch_cross,
    sketch_full,
    right_send,
    right_recv,
    right_part,
    right_cross,
    wide_send,
    wide_recv,
    half_send,
    half_recv,
    quarter_send,
    quarter_recv,
    piece_all,
    local_sem,
    send_sem,
    recv_sem,
):
    bf16, f32 = jnp.bfloat16, jnp.float32
    space, data = lax.axis_index("space"), lax.axis_index("dp")
    space_count, data_count = mode_send.shape[0], sketch_recv.shape[0]
    core, chip = lax.rem(data, 2), lax.div(data, 2)
    row_count, _, _ = grid_ref.shape
    slab = mode_send.shape[1] // row_count
    half = spectrum_ref.shape[0] // 2
    mode_local = KLON // space_count
    lat_count = row_count * space_count

    loads = []
    for index, (source, target) in enumerate(
        (
            (grid_hbm, grid_ref),
            (hidden_hbm, hidden_ref),
            (start_hbm, start_ref),
            (normed_hbm, normed_ref),
            (inner_hbm, inner_ref),
            (spectrum_hbm, spectrum_ref),
            (outer_hbm, outer_ref),
        )
    ):
        load = pltpu.make_async_copy(source, target, local_sem.at[index])
        load.start()
        loads.append(load)

    barrier = pltpu.get_barrier_semaphore()
    for step in range(1, space_count):
        pl.semaphore_signal(
            barrier,
            inc=1,
            device_id={"space": lax.rem(space + step, space_count)},
            device_id_type=pl.DeviceIdType.MESH,
        )
    for step in range(1, data_count):
        pl.semaphore_signal(
            barrier,
            inc=1,
            device_id={"dp": lax.rem(data + step, data_count)},
            device_id_type=pl.DeviceIdType.MESH,
        )

    pending = []

    def push(source, target, device):
        index = len(pending)
        copy = pltpu.make_async_remote_copy(
            src_ref=source,
            dst_ref=target,
            send_sem=send_sem.at[index],
            recv_sem=recv_sem.at[index],
            device_id=device,
            device_id_type=pl.DeviceIdType.MESH,
        )
        copy.start()
        pending.append(copy)
        return copy

    def over_space(source, target):
        copies = []
        for step in range(1, space_count):
            peer = lax.rem(space + step, space_count)
            copies.append(push(source(peer), target, {"space": peer}))
        return copies

    def over_data(source, target):
        copies = []
        for step in range(1, data_count):
            peer = lax.rem(data + step, data_count)
            copies.append(push(source(peer), target, {"dp": peer}))
        return copies

    def arrive(copies):
        for copy in copies:
            copy.wait_recv()

    loads[0].wait()
    for row in range(row_count):
        modes = mxu(lon_ref[...], grid_ref[row]).astype(bf16)
        for peer in range(space_count):
            mode_send[peer, row * slab : (row + 1) * slab, :] = modes[
                peer * slab : (peer + 1) * slab
            ]
    pl.semaphore_wait(barrier, space_count + data_count - 2)
    mode_copies = over_space(lambda peer: mode_send.at[peer], mode_recv.at[space])
    mode_recv[space] = mode_send[space]

    loads[1].wait()
    loads[2].wait()
    loads[3].wait()
    total = None
    for row in range(row_count):
        probe = mxu(hidden_ref[row], start_ref[...]).astype(bf16)
        term = mxu(probe, normed_ref[row], TN)
        total = term if total is None else total + term
    rank_part = sketch_local.shape[1]
    for peer in range(data_count):
        sketch_local[peer] = total[peer * rank_part : (peer + 1) * rank_part]
    sketch_copies = over_data(lambda peer: sketch_local.at[peer], sketch_recv.at[data])
    sketch_recv[data] = sketch_local[data]

    group = 4 * BS
    column = lax.broadcasted_iota(jnp.int32, (BS, group), 1)
    place = lax.broadcasted_iota(jnp.int32, (BS, group), 0)
    repeat = jnp.where(lax.rem(column, BS) == place, 1.0, 0.0).astype(bf16)
    loads[4].wait()
    loads[5].wait()
    loads[6].wait()
    for source, target in ((inner_ref, inner_wide), (outer_ref, outer_wide)):
        for block in range(2 * NB):
            rows = slice(block * BS, (block + 1) * BS)
            wide = mxu(source[rows, :], repeat)
            target[rows, :] = jnp.where(lax.div(column, BS) == block % 4, wide, 0.0).astype(bf16)

    def wide_weight(ref, part, index):
        first = (part * (NB // 4) + index) * group
        return ref[first : first + group, :]

    groups = [slice(index * group, (index + 1) * group) for index in range(NB // 4)]
    for index, lanes in enumerate(groups):
        values = spectrum_ref[:, lanes]
        by_real = mxu(values, wide_weight(inner_wide, 0, index))
        by_imag = mxu(values, wide_weight(inner_wide, 1, index))
        for rows, hidden in (
            (slice(0, half), by_real[:half] - by_imag[half:]),
            (slice(half, 2 * half), by_imag[:half] + by_real[half:]),
        ):
            cdf = 0.5 * (1.0 + lax.erf(hidden * math.sqrt(0.5)))
            density = jnp.exp(-0.5 * hidden * hidden) * (1.0 / math.sqrt(2.0 * math.pi))
            act_ref[rows, lanes] = (hidden * cdf).astype(bf16)
            slope_ref[rows, lanes] = cdf + hidden * density

    arrive(sketch_copies)
    part = sketch_recv[0]
    for peer in range(1, data_count):
        part = part + sketch_recv[peer]
    sketch_part[...] = part
    cross_copies = over_space(lambda peer: sketch_part, sketch_cross.at[space])
    sketch_cross[space] = part

    full = 2 * half
    lane = lax.broadcasted_iota(jnp.int32, (full, KLON), 1)
    row_id = lax.broadcasted_iota(jnp.int32, (full, KLON), 0)
    mode_id = space * mode_local + lax.rem(row_id, mode_local)
    own_cut = jnp.where(lane == mode_id, cutoff_ref[...].astype(f32), 0.0)
    cut = jnp.sum(own_cut, axis=1, keepdims=True)
    row_id = lax.broadcasted_iota(jnp.int32, (full, 1), 0)
    frequency = lax.rem(lax.div(row_id, mode_local), lat_count)
    size = jnp.where(frequency < lat_count // 2, frequency, lat_count - frequency).astype(f32)
    double = jnp.where(space * mode_local + lax.rem(row_id, mode_local) == 0, 1.0, 2.0)
    weight = jnp.where(size < cut, double, 0.0)

    arrive(cross_copies)
    part = sketch_cross[0]
    for peer in range(1, space_count):
        part = part + sketch_cross[peer]
    sketch_full[data] = part
    full_copies = over_data(lambda peer: sketch_full.at[data], sketch_full.at[data])

    arrive(mode_copies)
    arrived = mode_recv[...].reshape(full, D)
    cot_ref[...] = (mxu(lat_ref[...], arrived) * weight).astype(bf16)
    for index, lanes in enumerate(groups):
        values = cot_ref[:, lanes]
        by_real = mxu(values, wide_weight(outer_wide, 0, index), NT)
        by_imag = mxu(values, wide_weight(outer_wide, 1, index), NT)
        real = (by_real[:half] + by_imag[half:]) * slope_ref[:half, lanes]
        imag = (by_real[half:] - by_imag[:half]) * slope_ref[half:, lanes]
        hid_ref[:half, lanes] = real.astype(bf16)
        hid_ref[half:, lanes] = imag.astype(bf16)
        values = hid_ref[:, lanes]
        by_real = mxu(values, wide_weight(inner_wide, 0, index), NT)
        by_imag = mxu(values, wide_weight(inner_wide, 1, index), NT)
        xg_ref[:half, lanes] = (by_real[:half] + by_imag[half:]).astype(bf16)
        xg_ref[half:, lanes] = (by_real[half:] - by_imag[:half]).astype(bf16)
    back_send[...] = mxu(back_ref[...], xg_ref[...]).astype(bf16).reshape(back_send.shape)
    back_copies = over_space(lambda peer: back_send.at[peer], back_recv.at[space])
    back_recv[space] = back_send[space]

    lane_block = lax.div(lax.broadcasted_iota(jnp.int32, (BS, group), 1), BS)
    for first, left, right in ((0, spectrum_ref, hid_ref), (2, act_ref, cot_ref)):
        for index, lanes in enumerate(groups):
            values = left[:, lanes]
            turned = jnp.concatenate([right[half:, lanes], -right[:half, lanes]], axis=0)
            for part, other in ((0, right[:, lanes]), (1, turned)):
                product = mxu(values, other, TN)
                compact = jnp.zeros((BS, group), f32)
                for block in range(4):
                    compact = jnp.where(
                        lane_block == block, product[block * BS : (block + 1) * BS], compact
                    )
                compact = compact.astype(bf16)
                rows = slice((first + part) * BS, (first + part + 1) * BS)
                wide_send[0, index, rows, :] = compact[:, :256]
                wide_send[1, index, rows, :] = compact[:, 128:]
    pair = data + 1 - 2 * core
    core_copy = push(wide_send.at[1 - core], wide_recv, {"dp": pair})

    arrive(full_copies)
    sketch = sketch_full[...].reshape(data_count * rank_part, D)
    gram = lax.dot_general(
        sketch, sketch, NT, precision=HIGHEST, preferred_element_type=f32
    )
    rank = sketch.shape[0]
    rank_row = lax.broadcasted_iota(jnp.int32, (rank, 1), 0)
    for step in range(rank - 1):
        pivot = gram[step : step + 1, step : step + 1]
        ratio = jnp.where(rank_row > step, gram[:, step : step + 1] / pivot, 0.0)
        sketch = sketch - ratio * sketch[step : step + 1, :]
        gram = gram - ratio * gram[step : step + 1, :]
    eye = lax.broadcasted_iota(jnp.int32, (rank, rank), 0) == lax.broadcasted_iota(
        jnp.int32, (rank, rank), 1
    )
    diagonal = jnp.sum(jnp.where(eye, gram, 0.0), axis=1, keepdims=True)
    left_factor = sketch / jnp.sqrt(diagonal)
    left_out[...] = left_factor
    left_round = left_factor.astype(bf16)

    core_copy.wait_recv()
    mine = wide_send[core].astype(f32) + wide_recv[...].astype(f32)
    wide_recv[...] = mine.astype(bf16)
    chip_copy = push(wide_recv.at[1 - chip], half_recv, {"dp": lax.rem(data + 2, data_count)})

    total = None
    for row in range(row_count):
        mixed = mxu(left_round, normed_ref[row], NT).astype(bf16)
        term = mxu(mixed, hidden_ref[row])
        total = term if total is None else total + term
    total = total.astype(bf16)
    share = FF // (space_count * data_count)
    for owner in range(space_count * data_count):
        first = owner * share // 128 * 128
        right_send[owner % data_count, owner // data_count] = total[:, first : first + 256]
    right_copies = over_data(lambda peer: right_send.at[peer], right_recv.at[data])
    right_recv[data] = right_send[data]

    chip_copy.wait_recv()
    mine = wide_recv[chip].astype(f32) + half_recv[...].astype(f32)
    quarter_send[...] = mine.astype(bf16).reshape(quarter_send.shape)
    quarter_copies = over_space(lambda peer: quarter_send.at[peer], quarter_recv.at[space])
    quarter_recv[space] = quarter_send[space]

    arrive(right_copies)
    part = right_recv[0].astype(f32)
    for peer in range(1, data_count):
        part = part + right_recv[peer].astype(f32)
    right_part[...] = part.astype(bf16)
    last_copies = over_space(lambda peer: right_part.at[peer], right_cross.at[space])
    right_cross[space] = right_part[space]

    arrive(back_copies)
    arrived = back_recv[...].reshape(full, D)
    for row in range(row_count):
        grid_out[row] = (
            grid_ref[row].astype(f32) + mxu(spread_ref[row], arrived)
        ).astype(bf16)

    arrive(quarter_copies)
    part = quarter_recv[0].astype(f32)
    for peer in range(1, space_count):
        part = part + quarter_recv[peer].astype(f32)
    piece_all[space] = part.astype(bf16)
    piece_copies = over_space(lambda peer: piece_all.at[space], piece_all.at[space])

    arrive(last_copies)
    part = right_cross[0].astype(f32)
    for peer in range(1, space_count):
        part = part + right_cross[peer].astype(f32)
    tokens = data_count * lat_count * LON
    right_out[...] = part * (1.0 / math.sqrt(tokens))

    arrive(piece_copies)
    modes = data_count * lat_count * KLON
    weight_out[...] = piece_all[...].astype(f32).reshape(weight_out.shape) * (
        1.0 / math.sqrt(modes)
    )
    for copy in pending:
        copy.wait_send()


def fused_body(
    grad_mid, spectrum, filter_inner, filter_outer, cutoff, normed_mid, hidden_grad, power_start
):
    space_count = lax.axis_size("space")
    data_count = lax.axis_size("dp")
    row_count = grad_mid.shape[1]
    mode_local = KLON // space_count
    modes = 2 * row_count * space_count * mode_local
    rank = power_start.shape[1]
    bf16, f32 = jnp.bfloat16, jnp.float32
    lon_table, spread, lat_table, back_table = fused_tables(space_count, row_count)
    vmem = pl.BlockSpec(memory_space=pltpu.VMEM)
    anywhere = pl.BlockSpec(memory_space=pl.ANY)
    slab = (space_count, row_count * 2 * mode_local, D)
    copies = 5 * (space_count - 1) + 3 * (data_count - 1) + 2 + (space_count - 1)
    grid_out, weight_out, left_out, right_out = pl.pallas_call(
        fused_kernel,
        out_shape=(
            jax.ShapeDtypeStruct((row_count, LON, D), bf16),
            jax.ShapeDtypeStruct((4 * BS, 256), f32),
            jax.ShapeDtypeStruct((rank, D), f32),
            jax.ShapeDtypeStruct((rank, 256), f32),
        ),
        in_specs=[anywhere] * 4 + [vmem] + [anywhere] * 3 + [vmem] * 4,
        out_specs=(vmem,) * 4,
        scratch_shapes=[
            pltpu.VMEM((row_count, LON, D), bf16),
            pltpu.VMEM((modes, D), bf16),
            pltpu.VMEM((2 * NB * BS, BS), bf16),
            pltpu.VMEM((2 * NB * BS, BS), bf16),
            pltpu.VMEM((row_count, LON, D), bf16),
            pltpu.VMEM((row_count, LON, FF), bf16),
            pltpu.VMEM((FF, rank), bf16),
            pltpu.VMEM((2 * NB * BS, 4 * BS), bf16),
            pltpu.VMEM((2 * NB * BS, 4 * BS), bf16),
            pltpu.VMEM((modes, D), bf16),
            pltpu.VMEM((modes, D), f32),
            pltpu.VMEM((modes, D), bf16),
            pltpu.VMEM((modes, D), bf16),
            pltpu.VMEM((modes, D), bf16),
            pltpu.VMEM(slab, bf16),
            pltpu.VMEM(slab, bf16),
            pltpu.VMEM(slab, bf16),
            pltpu.VMEM(slab, bf16),
            pltpu.VMEM((data_count, rank // data_count, D), f32),
            pltpu.VMEM((data_count, rank // data_count, D), f32),
            pltpu.VMEM((rank // data_count, D), f32),
            pltpu.VMEM((space_count, rank // data_count, D), f32),
            pltpu.VMEM((data_count, rank // data_count, D), f32),
            pltpu.VMEM((data_count, space_count, rank, 256), bf16),
            pltpu.VMEM((data_count, space_count, rank, 256), bf16),
            pltpu.VMEM((space_count, rank, 256), bf16),
            pltpu.VMEM((space_count, rank, 256), bf16),
            pltpu.VMEM((2, 2, 4 * BS, 256), bf16),
            pltpu.VMEM((2, 4 * BS, 256), bf16),
            pltpu.VMEM((4 * BS, 256), bf16),
            pltpu.VMEM((4 * BS, 256), bf16),
            pltpu.VMEM((space_count, 4 * BS // space_count, 256), bf16),
            pltpu.VMEM((space_count, 4 * BS // space_count, 256), bf16),
            pltpu.VMEM((space_count, 4 * BS // space_count, 256), bf16),
            pltpu.SemaphoreType.DMA((7,)),
            pltpu.SemaphoreType.DMA((copies,)),
            pltpu.SemaphoreType.DMA((copies,)),
        ],
        compiler_params=pltpu.CompilerParams(
            collective_id=0, has_side_effects=True, vmem_limit_bytes=48 * 1024 * 1024
        ),
        name="fused_filter_sketch",
    )(
        grad_mid.reshape(row_count, LON, D),
        spectrum.reshape(modes, D),
        filter_inner.reshape(2 * NB * BS, BS),
        filter_outer.reshape(2 * NB * BS, BS),
        cutoff.reshape(1, KLON),
        normed_mid.reshape(row_count, LON, D),
        hidden_grad.reshape(row_count, LON, FF),
        power_start,
        lon_table,
        spread,
        lat_table,
        back_table,
    )
    odd = lax.rem(lax.axis_index("dp"), 2) == 1
    width = 2 * BS
    weights = jnp.where(odd, weight_out[:, 256 - width :], weight_out[:, :width])
    weights = weights.reshape(4, BS, 2, BS).transpose(0, 2, 1, 3)
    right = jnp.where(odd, right_out[:, 256 - width :], right_out[:, :width])
    return (grid_out.reshape(grad_mid.shape), weights[:2], weights[2:], left_out.T, right.T)


def solution(mesh):
    in_specs = (
        P(("groups", "dp"), "space", None, None),
        P(None, ("groups", "dp"), None, "space", None),
        P(),
        P(),
        P(),
        P(("groups", "dp"), "space", None, None),
        P(("groups", "dp"), "space", None, None),
        P(),
    )
    out_specs = (
        P(("groups", "dp"), "space", None, None),
        P("groups", "dp", None, None),
        P("groups", "dp", None, None),
        P("groups", None),
        P(("groups", "space", "dp"), None),
    )
    fits = mesh.shape["space"] == 4 and mesh.shape["dp"] == 4
    chosen = fused_body if fits else body
    return jax.shard_map(chosen, mesh=mesh, in_specs=in_specs, out_specs=out_specs, check_vma=False)
```

```python
import math

import jax
import jax.numpy as jnp
import numpy as np
from jax import lax
from jax.experimental import pallas as pl
from jax.experimental.pallas import tpu as pltpu
from jax.sharding import PartitionSpec as P

D = 768
NB = 8
BS = 96
FF = 3072
LON = 180
KLON = 64


HIGHEST = lax.Precision.HIGHEST


def angle_table(left_count, right_count, length):
    left_index = jnp.arange(left_count, dtype=jnp.int32)[:, None]
    right_index = jnp.arange(right_count, dtype=jnp.int32)[None, :]
    angles = (left_index * right_index % length).astype(jnp.float32) * (2.0 * math.pi / length)
    return (jnp.cos(angles), jnp.sin(angles))


def lon_forward(grid_values, cosine_table, sine_table, factor):
    real_part = jnp.einsum("srlc,kl->srkc", grid_values, cosine_table) * factor
    imag_part = -jnp.einsum("srlc,kl->srkc", grid_values, sine_table) * factor
    return jnp.stack([real_part, imag_part])


def lat_forward(complex_pair, cosine_table, sine_table):
    real_part = jnp.einsum(
        "jt,stkc->sjkc", cosine_table, complex_pair[0]
    ) + jnp.einsum("jt,stkc->sjkc", sine_table, complex_pair[1])
    imag_part = jnp.einsum(
        "jt,stkc->sjkc", cosine_table, complex_pair[1]
    ) - jnp.einsum("jt,stkc->sjkc", sine_table, complex_pair[0])
    return jnp.stack([real_part, imag_part])


def lat_adjoint(complex_pair, cosine_table, sine_table):
    real_part = jnp.einsum(
        "jt,sjkc->stkc", cosine_table, complex_pair[0]
    ) - jnp.einsum("jt,sjkc->stkc", sine_table, complex_pair[1])
    imag_part = jnp.einsum(
        "jt,sjkc->stkc", sine_table, complex_pair[0]
    ) + jnp.einsum("jt,sjkc->stkc", cosine_table, complex_pair[1])
    return jnp.stack([real_part, imag_part])


def lon_adjoint(complex_pair, cosine_table, sine_table, factor):
    summed = jnp.einsum(
        "srkc,kl->srlc", complex_pair[0], cosine_table
    ) - jnp.einsum("srkc,kl->srlc", complex_pair[1], sine_table)
    return summed * factor


def mode_weight(lat_count, first_mode, mode_count, cut_local):
    frequency = jnp.arange(lat_count, dtype=jnp.int32)
    signed = jnp.where(frequency < lat_count // 2, frequency, frequency - lat_count)
    mode_index = first_mode + jnp.arange(mode_count, dtype=jnp.int32)
    double = jnp.where(mode_index == 0, 1.0, 2.0)
    retained = jnp.abs(signed)[:, None] < cut_local[None, :]
    return jnp.where(retained, double[None, :], 0.0).astype(jnp.float32)


def complex_product(real_part, imag_part, weights):
    out_real = jnp.einsum("rbi,bio->rbo", real_part, weights[0]) - jnp.einsum(
        "rbi,bio->rbo", imag_part, weights[1]
    )
    out_imag = jnp.einsum("rbi,bio->rbo", real_part, weights[1]) + jnp.einsum(
        "rbi,bio->rbo", imag_part, weights[0]
    )
    return (out_real, out_imag)


def spectral_filter(real_part, imag_part, inner_weights, outer_weights):
    hidden_real, hidden_imag = complex_product(real_part, imag_part, inner_weights)
    return complex_product(
        jax.nn.gelu(hidden_real, approximate=False),
        jax.nn.gelu(hidden_imag, approximate=False),
        outer_weights,
    )


def filter_backward(spectrum_pair, cotangent, inner_weights, outer_weights):

    def shaped(values):
        return values.reshape(-1, NB, BS)

    outputs, pullback = jax.vjp(
        spectral_filter,
        shaped(spectrum_pair[0]),
        shaped(spectrum_pair[1]),
        inner_weights,
        outer_weights,
    )
    gradients = pullback((shaped(cotangent[0]), shaped(cotangent[1])))
    block_shape = spectrum_pair.shape[1:]
    mode_grad = jnp.stack([gradients[0].reshape(block_shape), gradients[1].reshape(block_shape)])
    return (mode_grad, gradients[2], gradients[3])


def orthonormal(sketch):
    gram_matrix = jnp.dot(sketch.T, sketch, precision=HIGHEST)
    cholesky_factor = jnp.linalg.cholesky(gram_matrix)
    return lax.linalg.triangular_solve(
        cholesky_factor, sketch, left_side=False, lower=True, transpose_a=True
    )


def body(
    grad_mid, spectrum, filter_inner, filter_outer, cutoff, normed_mid, hidden_grad, power_start
):
    space_count = lax.axis_size("space")
    data_count = lax.axis_size("dp")
    sample_count = grad_mid.shape[0]
    lat_count = grad_mid.shape[1] * space_count
    mode_local = KLON // space_count
    factor = 1.0 / math.sqrt(lat_count * LON)
    tokens_mid = normed_mid.reshape(-1, D)
    tokens_grad = hidden_grad.reshape(-1, FF)
    probe = jnp.dot(tokens_grad, power_start, preferred_element_type=jnp.float32).astype(
        jnp.bfloat16
    )
    sketch_local = jnp.dot(tokens_mid.T, probe, preferred_element_type=jnp.float32)
    sketch = lax.psum(sketch_local, ("space", "dp"))
    grad_float = grad_mid.astype(jnp.float32)
    lon_cos, lon_sin = angle_table(KLON, LON, LON)
    lat_cos, lat_sin = angle_table(lat_count, lat_count, lat_count)
    row_spectra = lon_forward(grad_float, lon_cos, lon_sin, factor)
    mode_values = lat_forward(
        lax.all_to_all(
            row_spectra.astype(jnp.bfloat16), "space", split_axis=3, concat_axis=2, tiled=True
        ).astype(jnp.float32),
        lat_cos,
        lat_sin,
    )
    first_mode = lax.axis_index("space") * mode_local
    cut_local = lax.dynamic_slice_in_dim(cutoff, first_mode, mode_local)
    weight = mode_weight(lat_count, first_mode, mode_local, cut_local)
    cotangent = mode_values * weight[None, None, :, :, None]
    mode_grad, inner_grad, outer_grad = filter_backward(
        spectrum.astype(jnp.float32),
        cotangent,
        filter_inner.astype(jnp.float32),
        filter_outer.astype(jnp.float32),
    )
    back = lat_adjoint(mode_grad, lat_cos, lat_sin)
    row_back = lax.all_to_all(
        back.astype(jnp.bfloat16), "space", split_axis=2, concat_axis=3, tiled=True
    ).astype(jnp.float32)
    spectral_grad = lon_adjoint(row_back, lon_cos, lon_sin, factor)
    grad_input = (grad_float + spectral_grad).astype(jnp.bfloat16)
    inner_grad, outer_grad = (
        lax.psum_scatter(
            inner_grad.astype(jnp.bfloat16), "dp", scatter_dimension=1, tiled=True
        ).astype(jnp.float32),
        lax.psum_scatter(
            outer_grad.astype(jnp.bfloat16), "dp", scatter_dimension=1, tiled=True
        ).astype(jnp.float32),
    )
    inner_grad, outer_grad = (
        lax.psum(inner_grad.astype(jnp.bfloat16), "space").astype(jnp.float32),
        lax.psum(outer_grad.astype(jnp.bfloat16), "space").astype(jnp.float32),
    )
    grad_factor = 1.0 / math.sqrt(sample_count * data_count * lat_count * KLON)
    left_factor = orthonormal(sketch)
    left_round = left_factor.astype(jnp.bfloat16)
    mixed = jnp.dot(tokens_mid, left_round, preferred_element_type=jnp.float32).astype(jnp.bfloat16)
    right_sum = lax.psum_scatter(
        jnp.dot(tokens_grad.T, mixed, preferred_element_type=jnp.float32),
        ("space", "dp"),
        scatter_dimension=0,
        tiled=True,
    )
    right_factor = right_sum * (1.0 / math.sqrt(sample_count * data_count * lat_count * LON))
    return (
        grad_input,
        inner_grad * grad_factor,
        outer_grad * grad_factor,
        left_factor,
        right_factor,
    )


def fused_tables(space_count, row_count):
    lat_count = space_count * row_count
    mode_local = KLON // space_count
    factor = 1.0 / math.sqrt(lat_count * LON)
    angle = (np.outer(np.arange(KLON), np.arange(LON)) % LON) * (2.0 * math.pi / LON)
    pair = np.stack([np.cos(angle), -np.sin(angle)]) * factor
    lon_table = (
        pair.reshape(2, space_count, mode_local, LON)
        .transpose(1, 0, 2, 3)
        .reshape(2 * KLON, LON)
    )
    spread = np.zeros((LON, row_count, space_count, row_count, 2 * mode_local))
    for row in range(row_count):
        spread[:, row, :, row, :] = lon_table.T.reshape(LON, space_count, 2 * mode_local)
    spread = spread.reshape(LON * row_count, space_count * row_count * 2 * mode_local)
    angle = (np.outer(np.arange(lat_count), np.arange(lat_count)) % lat_count) * (
        2.0 * math.pi / lat_count
    )
    cosine, sine = np.cos(angle), np.sin(angle)
    mix = np.stack([np.stack([cosine, sine], -1), np.stack([-sine, cosine], -1)])
    lat_table = np.einsum("ojti,kl->ojktil", mix, np.eye(mode_local)).reshape(
        2 * lat_count * mode_local, 2 * lat_count * mode_local
    )
    as_bf16 = lambda values: jnp.asarray(values.astype(np.float32), jnp.bfloat16)
    return as_bf16(spread.T.copy()), as_bf16(spread), as_bf16(lat_table), as_bf16(lat_table.T.copy())


NN = (((1,), (0,)), ((), ()))
NT = (((1,), (1,)), ((), ()))
TN = (((0,), (0,)), ((), ()))


def mxu(left, right, dims=NN):
    return lax.dot_general(left, right, dims, preferred_element_type=jnp.float32)


def fused_kernel(
    grid_hbm,
    spectrum_hbm,
    inner_hbm,
    outer_hbm,
    cutoff_ref,
    normed_hbm,
    hidden_hbm,
    start_hbm,
    lon_hbm,
    spread_hbm,
    lat_hbm,
    back_hbm,
    grid_hbm_out,
    weight_out,
    left_out,
    scale_out,
    right_out,
    lon_ref,
    spread_ref,
    lat_ref,
    back_ref,
    grid_out,
    grid_ref,
    spectrum_ref,
    inner_ref,
    outer_ref,
    normed_ref,
    hidden_ref,
    start_ref,
    inner_wide,
    outer_wide,
    act_ref,
    slope_ref,
    cot_ref,
    hid_ref,
    xg_ref,
    mode_send,
    mode_recv,
    back_send,
    back_recv,
    sketch_local,
    sketch_recv,
    sketch_part,
    sketch_cross,
    sketch_full,
    right_send,
    right_recv,
    right_part,
    right_cross,
    wide_send,
    wide_recv,
    half_send,
    half_recv,
    quarter_send,
    quarter_recv,
    piece_all,
    local_sem,
    send_sem,
    recv_sem,
):
    bf16, f32 = jnp.bfloat16, jnp.float32
    space, data = lax.axis_index("space"), lax.axis_index("dp")
    space_count, data_count = mode_send.shape[0], sketch_recv.shape[0]
    core, chip = lax.rem(data, 2), lax.div(data, 2)
    row_count = grid_ref.shape[2]
    token_count = grid_ref.shape[1] * row_count
    half = spectrum_ref.shape[0] // 2
    mode_local = KLON // space_count
    lat_count = row_count * space_count

    used = 0

    def load(source, target):
        nonlocal used
        copy = pltpu.make_async_copy(source, target, local_sem.at[used])
        copy.start()
        used += 1
        return copy

    def load_tokens(source, target):
        return [
            load(source.at[:, :, index * 128 : (index + 1) * 128], target.at[index])
            for index in range(target.shape[0])
        ]

    def finish(copies):
        for copy in copies:
            copy.wait()

    def tokens(ref):
        view = ref.reshape(ref.shape[0], token_count, 128)
        return jnp.concatenate([view[index] for index in range(ref.shape[0])], axis=1)

    grid_loads = load_tokens(grid_hbm, grid_ref) + [load(lon_hbm, lon_ref)]
    hidden_loads = load_tokens(hidden_hbm, hidden_ref) + [load(start_hbm, start_ref)]
    normed_loads = load_tokens(normed_hbm, normed_ref)
    other_loads = [
        load(source, target)
        for source, target in (
            (inner_hbm, inner_ref),
            (spectrum_hbm, spectrum_ref),
            (outer_hbm, outer_ref),
            (lat_hbm, lat_ref),
            (back_hbm, back_ref),
            (spread_hbm, spread_ref),
        )
    ]

    barrier = pltpu.get_barrier_semaphore()
    for step in range(1, space_count):
        pl.semaphore_signal(
            barrier,
            inc=1,
            device_id={"space": lax.rem(space + step, space_count)},
            device_id_type=pl.DeviceIdType.MESH,
        )
    for step in range(1, data_count):
        pl.semaphore_signal(
            barrier,
            inc=1,
            device_id={"dp": lax.rem(data + step, data_count)},
            device_id_type=pl.DeviceIdType.MESH,
        )

    pending = []

    def push(source, target, device):
        index = len(pending)
        copy = pltpu.make_async_remote_copy(
            src_ref=source,
            dst_ref=target,
            send_sem=send_sem.at[index],
            recv_sem=recv_sem.at[index],
            device_id=device,
            device_id_type=pl.DeviceIdType.MESH,
        )
        copy.start()
        pending.append(copy)
        return copy

    def over_space(source, target):
        copies = []
        for step in range(1, space_count):
            peer = lax.rem(space + step, space_count)
            copies.append(push(source(peer), target, {"space": peer}))
        return copies

    def over_data(source, target):
        copies = []
        for step in range(1, data_count):
            peer = lax.rem(data + step, data_count)
            copies.append(push(source(peer), target, {"dp": peer}))
        return copies

    def arrive(copies):
        for copy in copies:
            copy.wait_recv()

    finish(grid_loads)
    mode_send[...] = mxu(lon_ref[...], tokens(grid_ref)).astype(bf16).reshape(mode_send.shape)
    pl.semaphore_wait(barrier, space_count + data_count - 2)
    mode_copies = over_space(lambda peer: mode_send.at[peer], mode_recv.at[space])
    mode_recv[space] = mode_send[space]

    finish(hidden_loads)
    probe = mxu(tokens(hidden_ref), start_ref[...], NT).astype(bf16)
    finish(normed_loads)
    total = mxu(probe, tokens(normed_ref), TN)
    rank_part = sketch_local.shape[1]
    for peer in range(data_count):
        sketch_local[peer] = total[peer * rank_part : (peer + 1) * rank_part]
    sketch_copies = over_data(lambda peer: sketch_local.at[peer], sketch_recv.at[data])
    sketch_recv[data] = sketch_local[data]

    group = 4 * BS
    column = lax.broadcasted_iota(jnp.int32, (BS, group), 1)
    place = lax.broadcasted_iota(jnp.int32, (BS, group), 0)
    repeat = jnp.where(lax.rem(column, BS) == place, 1.0, 0.0).astype(bf16)
    finish(other_loads)
    for source, target in ((inner_ref, inner_wide), (outer_ref, outer_wide)):
        for block in range(2 * NB):
            rows = slice(block * BS, (block + 1) * BS)
            wide = mxu(source[rows, :], repeat)
            target[rows, :] = jnp.where(lax.div(column, BS) == block % 4, wide, 0.0).astype(bf16)

    def wide_weight(ref, part, index):
        first = (part * (NB // 4) + index) * group
        return ref[first : first + group, :]

    groups = [slice(index * group, (index + 1) * group) for index in range(NB // 4)]
    for index, lanes in enumerate(groups):
        values = spectrum_ref[:, lanes]
        by_real = mxu(values, wide_weight(inner_wide, 0, index))
        by_imag = mxu(values, wide_weight(inner_wide, 1, index))
        for rows, hidden in (
            (slice(0, half), by_real[:half] - by_imag[half:]),
            (slice(half, 2 * half), by_imag[:half] + by_real[half:]),
        ):
            cdf = 0.5 * (1.0 + lax.erf(hidden * math.sqrt(0.5)))
            density = jnp.exp(-0.5 * hidden * hidden) * (1.0 / math.sqrt(2.0 * math.pi))
            act_ref[rows, lanes] = (hidden * cdf).astype(bf16)
            slope_ref[rows, lanes] = cdf + hidden * density

    arrive(sketch_copies)
    part = sketch_recv[0]
    for peer in range(1, data_count):
        part = part + sketch_recv[peer]
    sketch_part[...] = part
    cross_copies = over_space(lambda peer: sketch_part, sketch_cross.at[space])
    sketch_cross[space] = part

    full = 2 * half
    lane = lax.broadcasted_iota(jnp.int32, (full, KLON), 1)
    row_id = lax.broadcasted_iota(jnp.int32, (full, KLON), 0)
    mode_id = space * mode_local + lax.rem(row_id, mode_local)
    own_cut = jnp.where(lane == mode_id, cutoff_ref[...].astype(f32), 0.0)
    cut = jnp.sum(own_cut, axis=1, keepdims=True)
    row_id = lax.broadcasted_iota(jnp.int32, (full, 1), 0)
    frequency = lax.rem(lax.div(row_id, mode_local), lat_count)
    size = jnp.where(frequency < lat_count // 2, frequency, lat_count - frequency).astype(f32)
    double = jnp.where(space * mode_local + lax.rem(row_id, mode_local) == 0, 1.0, 2.0)
    weight = jnp.where(size < cut, double, 0.0)

    arrive(cross_copies)
    part = sketch_cross[0]
    for peer in range(1, space_count):
        part = part + sketch_cross[peer]
    sketch_full[data] = part
    full_copies = over_data(lambda peer: sketch_full.at[data], sketch_full.at[data])

    arrive(mode_copies)
    arrived = mode_recv[...].reshape(full, D)
    cot_ref[...] = (mxu(lat_ref[...], arrived) * weight).astype(bf16)
    for index, lanes in enumerate(groups):
        values = cot_ref[:, lanes]
        by_real = mxu(values, wide_weight(outer_wide, 0, index), NT)
        by_imag = mxu(values, wide_weight(outer_wide, 1, index), NT)
        real = (by_real[:half] + by_imag[half:]) * slope_ref[:half, lanes]
        imag = (by_real[half:] - by_imag[:half]) * slope_ref[half:, lanes]
        hid_ref[:half, lanes] = real.astype(bf16)
        hid_ref[half:, lanes] = imag.astype(bf16)
        values = hid_ref[:, lanes]
        by_real = mxu(values, wide_weight(inner_wide, 0, index), NT)
        by_imag = mxu(values, wide_weight(inner_wide, 1, index), NT)
        xg_ref[:half, lanes] = (by_real[:half] + by_imag[half:]).astype(bf16)
        xg_ref[half:, lanes] = (by_real[half:] - by_imag[:half]).astype(bf16)
    back_send[...] = mxu(back_ref[...], xg_ref[...]).astype(bf16).reshape(back_send.shape)
    back_copies = over_space(lambda peer: back_send.at[peer], back_recv.at[space])
    back_recv[space] = back_send[space]

    lane_block = lax.div(lax.broadcasted_iota(jnp.int32, (BS, group), 1), BS)
    for first, left, right in ((0, spectrum_ref, hid_ref), (2, act_ref, cot_ref)):
        for index, lanes in enumerate(groups):
            values = left[:, lanes]
            turned = jnp.concatenate([right[half:, lanes], -right[:half, lanes]], axis=0)
            for part, other in ((0, right[:, lanes]), (1, turned)):
                product = mxu(values, other, TN)
                compact = jnp.zeros((BS, group), f32)
                for block in range(4):
                    compact = jnp.where(
                        lane_block == block, product[block * BS : (block + 1) * BS], compact
                    )
                compact = compact.astype(bf16)
                rows = slice((first + part) * BS, (first + part + 1) * BS)
                wide_send[0, index, rows, :] = compact[:, :256]
                wide_send[1, index, rows, :] = compact[:, 128:]
    pair = data + 1 - 2 * core
    core_copy = push(wide_send.at[1 - core], wide_recv, {"dp": pair})

    arrive(full_copies)
    sketch = sketch_full[...].reshape(data_count * rank_part, D)
    gram = lax.dot_general(
        sketch, sketch, NT, precision=HIGHEST, preferred_element_type=f32
    )
    rank = sketch.shape[0]
    rank_row = lax.broadcasted_iota(jnp.int32, (rank, 1), 0)
    for step in range(rank - 1):
        pivot = gram[step : step + 1, step : step + 1]
        ratio = jnp.where(rank_row > step, gram[:, step : step + 1] / pivot, 0.0)
        sketch = sketch - ratio * sketch[step : step + 1, :]
        gram = gram - ratio * gram[step : step + 1, :]
    eye = lax.broadcasted_iota(jnp.int32, (rank, rank), 0) == lax.broadcasted_iota(
        jnp.int32, (rank, rank), 1
    )
    diagonal = jnp.sum(jnp.where(eye, gram, 0.0), axis=1, keepdims=True)
    scale = 1.0 / jnp.sqrt(diagonal)
    left_out[...] = sketch
    scale_out[...] = scale
    left_round = (sketch * scale).astype(bf16)

    core_copy.wait_recv()
    mine = wide_send[core].astype(f32) + wide_recv[...].astype(f32)
    wide_recv[...] = mine.astype(bf16)
    chip_copy = push(wide_recv.at[1 - chip], half_recv, {"dp": lax.rem(data + 2, data_count)})

    mixed = mxu(left_round, tokens(normed_ref), NT).astype(bf16)
    total = mxu(mixed, tokens(hidden_ref)).astype(bf16)
    share = FF // (space_count * data_count)
    for owner in range(space_count * data_count):
        first = owner * share // 128 * 128
        right_send[owner % data_count, owner // data_count] = total[:, first : first + 256]
    right_copies = over_data(lambda peer: right_send.at[peer], right_recv.at[data])
    right_recv[data] = right_send[data]

    chip_copy.wait_recv()
    mine = wide_recv[chip].astype(f32) + half_recv[...].astype(f32)
    quarter_send[...] = mine.astype(bf16).reshape(quarter_send.shape)
    quarter_copies = over_space(lambda peer: quarter_send.at[peer], quarter_recv.at[space])
    quarter_recv[space] = quarter_send[space]

    arrive(right_copies)
    part = right_recv[0].astype(f32)
    for peer in range(1, data_count):
        part = part + right_recv[peer].astype(f32)
    right_part[...] = part.astype(bf16)
    last_copies = over_space(lambda peer: right_part.at[peer], right_cross.at[space])
    right_cross[space] = right_part[space]

    arrive(back_copies)
    arrived = back_recv[...].reshape(full, D)
    grid_view = grid_out.reshape(grid_out.shape[0], token_count, 128)
    result = (tokens(grid_ref).astype(f32) + mxu(spread_ref[...], arrived)).astype(bf16)
    for index in range(grid_out.shape[0]):
        grid_view[index] = result[:, index * 128 : (index + 1) * 128]
    stores = [
        load(grid_out.at[index], grid_hbm_out.at[:, :, index * 128 : (index + 1) * 128])
        for index in range(grid_out.shape[0])
    ]

    arrive(quarter_copies)
    part = quarter_recv[0].astype(f32)
    for peer in range(1, space_count):
        part = part + quarter_recv[peer].astype(f32)
    piece_all[space] = part.astype(bf16)
    piece_copies = over_space(lambda peer: piece_all.at[space], piece_all.at[space])

    arrive(last_copies)
    part = right_cross[0].astype(f32)
    for peer in range(1, space_count):
        part = part + right_cross[peer].astype(f32)
    part = jnp.where(core == 1, pltpu.roll(part, 192, 1), part)
    right_out[...] = part[:, : 2 * BS]

    arrive(piece_copies)
    for index in range(space_count):
        part = piece_all[index].astype(f32)
        part = jnp.where(core == 1, pltpu.roll(part, 192, 1), part)
        weight_out[index, 0] = part[:, :BS]
        weight_out[index, 1] = pltpu.roll(part, 256 - BS, 1)[:, :BS]
    finish(stores)
    for copy in pending:
        copy.wait_send()


def fused_body(
    grad_mid, spectrum, filter_inner, filter_outer, cutoff, normed_mid, hidden_grad, power_start
):
    space_count = lax.axis_size("space")
    data_count = lax.axis_size("dp")
    row_count = grad_mid.shape[1]
    mode_local = KLON // space_count
    modes = 2 * row_count * space_count * mode_local
    rank = power_start.shape[1]
    bf16, f32 = jnp.bfloat16, jnp.float32
    lon_table, spread, lat_table, back_table = fused_tables(space_count, row_count)
    vmem = pl.BlockSpec(memory_space=pltpu.VMEM)
    anywhere = pl.BlockSpec(memory_space=pl.ANY)
    slab = (space_count, row_count * 2 * mode_local, D)
    copies = 5 * (space_count - 1) + 3 * (data_count - 1) + 2 + (space_count - 1)
    grid_shape = (D // 128, LON, row_count, 128)
    grid_out, weight_out, left_out, scale_out, right_out = pl.pallas_call(
        fused_kernel,
        out_shape=(
            jax.ShapeDtypeStruct((LON, row_count, D), bf16),
            jax.ShapeDtypeStruct((4, 2, BS, BS), f32),
            jax.ShapeDtypeStruct((rank, D), f32),
            jax.ShapeDtypeStruct((rank, 1), f32),
            jax.ShapeDtypeStruct((rank, 2 * BS), f32),
        ),
        in_specs=[anywhere] * 4 + [vmem] + [anywhere] * 7,
        out_specs=(anywhere,) + (vmem,) * 4,
        scratch_shapes=[
            pltpu.VMEM((modes, LON * row_count), bf16),
            pltpu.VMEM((LON * row_count, modes), bf16),
            pltpu.VMEM((modes, modes), bf16),
            pltpu.VMEM((modes, modes), bf16),
            pltpu.VMEM(grid_shape, bf16),
            pltpu.VMEM(grid_shape, bf16),
            pltpu.VMEM((modes, D), bf16),
            pltpu.VMEM((2 * NB * BS, BS), bf16),
            pltpu.VMEM((2 * NB * BS, BS), bf16),
            pltpu.VMEM(grid_shape, bf16),
            pltpu.VMEM((FF // 128, LON, row_count, 128), bf16),
            pltpu.VMEM((rank, FF), bf16),
            pltpu.VMEM((2 * NB * BS, 4 * BS), bf16),
            pltpu.VMEM((2 * NB * BS, 4 * BS), bf16),
            pltpu.VMEM((modes, D), bf16),
            pltpu.VMEM((modes, D), f32),
            pltpu.VMEM((modes, D), bf16),
            pltpu.VMEM((modes, D), bf16),
            pltpu.VMEM((modes, D), bf16),
            pltpu.VMEM(slab, bf16),
            pltpu.VMEM(slab, bf16),
            pltpu.VMEM(slab, bf16),
            pltpu.VMEM(slab, bf16),
            pltpu.VMEM((data_count, rank // data_count, D), f32),
            pltpu.VMEM((data_count, rank // data_count, D), f32),
            pltpu.VMEM((rank // data_count, D), f32),
            pltpu.VMEM((space_count, rank // data_count, D), f32),
            pltpu.VMEM((data_count, rank // data_count, D), f32),
            pltpu.VMEM((data_count, space_count, rank, 256), bf16),
            pltpu.VMEM((data_count, space_count, rank, 256), bf16),
            pltpu.VMEM((space_count, rank, 256), bf16),
            pltpu.VMEM((space_count, rank, 256), bf16),
            pltpu.VMEM((2, 2, 4 * BS, 256), bf16),
            pltpu.VMEM((2, 4 * BS, 256), bf16),
            pltpu.VMEM((4 * BS, 256), bf16),
            pltpu.VMEM((4 * BS, 256), bf16),
            pltpu.VMEM((space_count, 4 * BS // space_count, 256), bf16),
            pltpu.VMEM((space_count, 4 * BS // space_count, 256), bf16),
            pltpu.VMEM((space_count, 4 * BS // space_count, 256), bf16),
            pltpu.SemaphoreType.DMA((3 * (D // 128) + FF // 128 + 8,)),
            pltpu.SemaphoreType.DMA((copies,)),
            pltpu.SemaphoreType.DMA((copies,)),
        ],
        compiler_params=pltpu.CompilerParams(
            collective_id=0, has_side_effects=True, vmem_limit_bytes=60 * 1024 * 1024
        ),
        name="fused_filter_sketch",
    )(
        grad_mid.transpose(0, 2, 1, 3).reshape(LON, row_count, D),
        spectrum.reshape(modes, D),
        filter_inner.reshape(2 * NB * BS, BS),
        filter_outer.reshape(2 * NB * BS, BS),
        cutoff.reshape(1, KLON),
        normed_mid.transpose(0, 2, 1, 3).reshape(LON, row_count, D),
        hidden_grad.transpose(0, 2, 1, 3).reshape(LON, row_count, FF),
        power_start.T,
        lon_table,
        spread,
        lat_table,
        back_table,
    )
    samples = data_count * row_count * space_count
    weights = weight_out * (1.0 / math.sqrt(samples * KLON))
    left = (left_out * scale_out).T
    right = right_out.T * (1.0 / math.sqrt(samples * LON))
    grid = grid_out.reshape(1, LON, row_count, D).transpose(0, 2, 1, 3)
    return (grid, weights[:2], weights[2:], left, right)


def solution(mesh):
    in_specs = (
        P(("groups", "dp"), "space", None, None),
        P(None, ("groups", "dp"), None, "space", None),
        P(),
        P(),
        P(),
        P(("groups", "dp"), "space", None, None),
        P(("groups", "dp"), "space", None, None),
        P(),
    )
    out_specs = (
        P(("groups", "dp"), "space", None, None),
        P("groups", "dp", None, None),
        P("groups", "dp", None, None),
        P("groups", None),
        P(("groups", "space", "dp"), None),
    )
    fits = mesh.shape["space"] == 4 and mesh.shape["dp"] == 4
    chosen = fused_body if fits else body
    return jax.shard_map(chosen, mesh=mesh, in_specs=in_specs, out_specs=out_specs, check_vma=False)
```

```python
import math

import jax
import jax.numpy as jnp
import numpy as np
from jax import lax
from jax.experimental import pallas as pl
from jax.experimental.pallas import tpu as pltpu
from jax.sharding import PartitionSpec as P

D = 768
NB = 8
BS = 96
FF = 3072
LON = 180
KLON = 64


HIGHEST = lax.Precision.HIGHEST


def angle_table(left_count, right_count, length):
    left_index = jnp.arange(left_count, dtype=jnp.int32)[:, None]
    right_index = jnp.arange(right_count, dtype=jnp.int32)[None, :]
    angles = (left_index * right_index % length).astype(jnp.float32) * (2.0 * math.pi / length)
    return (jnp.cos(angles), jnp.sin(angles))


def lon_forward(grid_values, cosine_table, sine_table, factor):
    real_part = jnp.einsum("srlc,kl->srkc", grid_values, cosine_table) * factor
    imag_part = -jnp.einsum("srlc,kl->srkc", grid_values, sine_table) * factor
    return jnp.stack([real_part, imag_part])


def lat_forward(complex_pair, cosine_table, sine_table):
    real_part = jnp.einsum(
        "jt,stkc->sjkc", cosine_table, complex_pair[0]
    ) + jnp.einsum("jt,stkc->sjkc", sine_table, complex_pair[1])
    imag_part = jnp.einsum(
        "jt,stkc->sjkc", cosine_table, complex_pair[1]
    ) - jnp.einsum("jt,stkc->sjkc", sine_table, complex_pair[0])
    return jnp.stack([real_part, imag_part])


def lat_adjoint(complex_pair, cosine_table, sine_table):
    real_part = jnp.einsum(
        "jt,sjkc->stkc", cosine_table, complex_pair[0]
    ) - jnp.einsum("jt,sjkc->stkc", sine_table, complex_pair[1])
    imag_part = jnp.einsum(
        "jt,sjkc->stkc", sine_table, complex_pair[0]
    ) + jnp.einsum("jt,sjkc->stkc", cosine_table, complex_pair[1])
    return jnp.stack([real_part, imag_part])


def lon_adjoint(complex_pair, cosine_table, sine_table, factor):
    summed = jnp.einsum(
        "srkc,kl->srlc", complex_pair[0], cosine_table
    ) - jnp.einsum("srkc,kl->srlc", complex_pair[1], sine_table)
    return summed * factor


def mode_weight(lat_count, first_mode, mode_count, cut_local):
    frequency = jnp.arange(lat_count, dtype=jnp.int32)
    signed = jnp.where(frequency < lat_count // 2, frequency, frequency - lat_count)
    mode_index = first_mode + jnp.arange(mode_count, dtype=jnp.int32)
    double = jnp.where(mode_index == 0, 1.0, 2.0)
    retained = jnp.abs(signed)[:, None] < cut_local[None, :]
    return jnp.where(retained, double[None, :], 0.0).astype(jnp.float32)


def complex_product(real_part, imag_part, weights):
    out_real = jnp.einsum("rbi,bio->rbo", real_part, weights[0]) - jnp.einsum(
        "rbi,bio->rbo", imag_part, weights[1]
    )
    out_imag = jnp.einsum("rbi,bio->rbo", real_part, weights[1]) + jnp.einsum(
        "rbi,bio->rbo", imag_part, weights[0]
    )
    return (out_real, out_imag)


def spectral_filter(real_part, imag_part, inner_weights, outer_weights):
    hidden_real, hidden_imag = complex_product(real_part, imag_part, inner_weights)
    return complex_product(
        jax.nn.gelu(hidden_real, approximate=False),
        jax.nn.gelu(hidden_imag, approximate=False),
        outer_weights,
    )


def filter_backward(spectrum_pair, cotangent, inner_weights, outer_weights):

    def shaped(values):
        return values.reshape(-1, NB, BS)

    outputs, pullback = jax.vjp(
        spectral_filter,
        shaped(spectrum_pair[0]),
        shaped(spectrum_pair[1]),
        inner_weights,
        outer_weights,
    )
    gradients = pullback((shaped(cotangent[0]), shaped(cotangent[1])))
    block_shape = spectrum_pair.shape[1:]
    mode_grad = jnp.stack([gradients[0].reshape(block_shape), gradients[1].reshape(block_shape)])
    return (mode_grad, gradients[2], gradients[3])


def orthonormal(sketch):
    gram_matrix = jnp.dot(sketch.T, sketch, precision=HIGHEST)
    cholesky_factor = jnp.linalg.cholesky(gram_matrix)
    return lax.linalg.triangular_solve(
        cholesky_factor, sketch, left_side=False, lower=True, transpose_a=True
    )


def body(
    grad_mid, spectrum, filter_inner, filter_outer, cutoff, normed_mid, hidden_grad, power_start
):
    space_count = lax.axis_size("space")
    data_count = lax.axis_size("dp")
    sample_count = grad_mid.shape[0]
    lat_count = grad_mid.shape[1] * space_count
    mode_local = KLON // space_count
    factor = 1.0 / math.sqrt(lat_count * LON)
    tokens_mid = normed_mid.reshape(-1, D)
    tokens_grad = hidden_grad.reshape(-1, FF)
    probe = jnp.dot(tokens_grad, power_start, preferred_element_type=jnp.float32).astype(
        jnp.bfloat16
    )
    sketch_local = jnp.dot(tokens_mid.T, probe, preferred_element_type=jnp.float32)
    sketch = lax.psum(sketch_local, ("space", "dp"))
    grad_float = grad_mid.astype(jnp.float32)
    lon_cos, lon_sin = angle_table(KLON, LON, LON)
    lat_cos, lat_sin = angle_table(lat_count, lat_count, lat_count)
    row_spectra = lon_forward(grad_float, lon_cos, lon_sin, factor)
    mode_values = lat_forward(
        lax.all_to_all(
            row_spectra.astype(jnp.bfloat16), "space", split_axis=3, concat_axis=2, tiled=True
        ).astype(jnp.float32),
        lat_cos,
        lat_sin,
    )
    first_mode = lax.axis_index("space") * mode_local
    cut_local = lax.dynamic_slice_in_dim(cutoff, first_mode, mode_local)
    weight = mode_weight(lat_count, first_mode, mode_local, cut_local)
    cotangent = mode_values * weight[None, None, :, :, None]
    mode_grad, inner_grad, outer_grad = filter_backward(
        spectrum.astype(jnp.float32),
        cotangent,
        filter_inner.astype(jnp.float32),
        filter_outer.astype(jnp.float32),
    )
    back = lat_adjoint(mode_grad, lat_cos, lat_sin)
    row_back = lax.all_to_all(
        back.astype(jnp.bfloat16), "space", split_axis=2, concat_axis=3, tiled=True
    ).astype(jnp.float32)
    spectral_grad = lon_adjoint(row_back, lon_cos, lon_sin, factor)
    grad_input = (grad_float + spectral_grad).astype(jnp.bfloat16)
    inner_grad, outer_grad = (
        lax.psum_scatter(
            inner_grad.astype(jnp.bfloat16), "dp", scatter_dimension=1, tiled=True
        ).astype(jnp.float32),
        lax.psum_scatter(
            outer_grad.astype(jnp.bfloat16), "dp", scatter_dimension=1, tiled=True
        ).astype(jnp.float32),
    )
    inner_grad, outer_grad = (
        lax.psum(inner_grad.astype(jnp.bfloat16), "space").astype(jnp.float32),
        lax.psum(outer_grad.astype(jnp.bfloat16), "space").astype(jnp.float32),
    )
    grad_factor = 1.0 / math.sqrt(sample_count * data_count * lat_count * KLON)
    left_factor = orthonormal(sketch)
    left_round = left_factor.astype(jnp.bfloat16)
    mixed = jnp.dot(tokens_mid, left_round, preferred_element_type=jnp.float32).astype(jnp.bfloat16)
    right_sum = lax.psum_scatter(
        jnp.dot(tokens_grad.T, mixed, preferred_element_type=jnp.float32),
        ("space", "dp"),
        scatter_dimension=0,
        tiled=True,
    )
    right_factor = right_sum * (1.0 / math.sqrt(sample_count * data_count * lat_count * LON))
    return (
        grad_input,
        inner_grad * grad_factor,
        outer_grad * grad_factor,
        left_factor,
        right_factor,
    )


def fused_tables(space_count, row_count):
    lat_count = space_count * row_count
    mode_local = KLON // space_count
    factor = 1.0 / math.sqrt(lat_count * LON)
    angle = (np.outer(np.arange(KLON), np.arange(LON)) % LON) * (2.0 * math.pi / LON)
    pair = np.stack([np.cos(angle), -np.sin(angle)]) * factor
    lon_table = (
        pair.reshape(2, space_count, mode_local, LON)
        .transpose(1, 0, 2, 3)
        .reshape(2 * KLON, LON)
    )
    spread = np.zeros((LON, row_count, space_count, row_count, 2 * mode_local))
    for row in range(row_count):
        spread[:, row, :, row, :] = lon_table.T.reshape(LON, space_count, 2 * mode_local)
    spread = spread.reshape(LON * row_count, space_count * row_count * 2 * mode_local)
    angle = (np.outer(np.arange(lat_count), np.arange(lat_count)) % lat_count) * (
        2.0 * math.pi / lat_count
    )
    cosine, sine = np.cos(angle), np.sin(angle)
    mix = np.stack([np.stack([cosine, sine], -1), np.stack([-sine, cosine], -1)])
    lat_table = np.einsum("ojti,kl->ojktil", mix, np.eye(mode_local)).reshape(
        2 * lat_count * mode_local, 2 * lat_count * mode_local
    )
    as_bf16 = lambda values: jnp.asarray(values.astype(np.float32), jnp.bfloat16)
    return as_bf16(spread.T.copy()), as_bf16(spread), as_bf16(lat_table), as_bf16(lat_table.T.copy())


NN = (((1,), (0,)), ((), ()))
NT = (((1,), (1,)), ((), ()))
TN = (((0,), (0,)), ((), ()))


def mxu(left, right, dims=NN):
    return lax.dot_general(left, right, dims, preferred_element_type=jnp.float32)


def fused_kernel(
    grid_hbm,
    spectrum_hbm,
    inner_hbm,
    outer_hbm,
    cutoff_ref,
    normed_hbm,
    hidden_hbm,
    start_hbm,
    lon_hbm,
    spread_hbm,
    lat_hbm,
    back_hbm,
    grid_hbm_out,
    inner_out,
    outer_out,
    left_out,
    right_out,
    lon_ref,
    spread_ref,
    lat_ref,
    back_ref,
    grid_out,
    grid_ref,
    spectrum_ref,
    inner_ref,
    outer_ref,
    normed_ref,
    hidden_ref,
    start_ref,
    inner_wide,
    outer_wide,
    act_ref,
    slope_ref,
    cot_ref,
    hid_ref,
    xg_ref,
    mode_send,
    mode_recv,
    back_send,
    back_recv,
    sketch_local,
    sketch_recv,
    sketch_part,
    sketch_cross,
    sketch_full,
    right_send,
    right_recv,
    right_part,
    right_cross,
    wide_send,
    wide_recv,
    half_recv,
    quarter_send,
    quarter_recv,
    piece_all,
    local_sem,
    send_sem,
    recv_sem,
):
    bf16, f32 = jnp.bfloat16, jnp.float32
    space, data = lax.axis_index("space"), lax.axis_index("dp")
    space_count, data_count = mode_send.shape[1], sketch_recv.shape[0]
    core, chip = lax.rem(data, 2), lax.div(data, 2)
    row_count = grid_ref.shape[2]
    token_count = grid_ref.shape[1] * row_count
    half = spectrum_ref.shape[0] // 2
    mode_local = KLON // space_count
    lat_count = row_count * space_count

    used = 0

    def load(source, target):
        nonlocal used
        copy = pltpu.make_async_copy(source, target, local_sem.at[used])
        copy.start()
        used += 1
        return copy

    def load_tokens(source, target):
        return [
            load(source.at[:, :, index * 128 : (index + 1) * 128], target.at[index])
            for index in range(target.shape[0])
        ]

    def finish(copies):
        for copy in copies:
            copy.wait()

    def tokens(ref):
        view = ref.reshape(ref.shape[0], token_count, 128)
        return jnp.concatenate([view[index] for index in range(ref.shape[0])], axis=1)

    grid_loads = load_tokens(grid_hbm, grid_ref) + [load(lon_hbm, lon_ref)]
    hidden_loads = load_tokens(hidden_hbm, hidden_ref) + [load(start_hbm, start_ref)]
    normed_loads = load_tokens(normed_hbm, normed_ref)
    other_loads = [
        load(source, target)
        for source, target in (
            (inner_hbm, inner_ref),
            (spectrum_hbm, spectrum_ref),
            (outer_hbm, outer_ref),
            (lat_hbm, lat_ref),
            (back_hbm, back_ref),
            (spread_hbm, spread_ref),
        )
    ]

    barrier = pltpu.get_barrier_semaphore()
    for step in range(1, space_count):
        pl.semaphore_signal(
            barrier,
            inc=1,
            device_id={"space": lax.rem(space + step, space_count)},
            device_id_type=pl.DeviceIdType.MESH,
        )
    for step in range(1, data_count):
        pl.semaphore_signal(
            barrier,
            inc=1,
            device_id={"dp": lax.rem(data + step, data_count)},
            device_id_type=pl.DeviceIdType.MESH,
        )

    pending = []

    def push(source, target, device):
        index = len(pending)
        copy = pltpu.make_async_remote_copy(
            src_ref=source,
            dst_ref=target,
            send_sem=send_sem.at[index],
            recv_sem=recv_sem.at[index],
            device_id=device,
            device_id_type=pl.DeviceIdType.MESH,
        )
        copy.start()
        pending.append(copy)
        return copy

    def over_space(source, target):
        copies = []
        for step in range(1, space_count):
            peer = lax.rem(space + step, space_count)
            copies.append(push(source(peer), target, {"space": peer}))
        return copies

    def over_data(source, target):
        copies = []
        for step in range(1, data_count):
            peer = lax.rem(data + step, data_count)
            copies.append(push(source(peer), target, {"dp": peer}))
        return copies

    def arrive(copies):
        for copy in copies:
            copy.wait_recv()

    group = 4 * BS
    groups = [slice(index * group, (index + 1) * group) for index in range(NB // 4)]
    finish(grid_loads)
    grid_tokens = tokens(grid_ref)
    mode_copies = []
    for index, lanes in enumerate(groups):
        modes = mxu(lon_ref[...], grid_tokens[:, lanes]).astype(bf16)
        mode_send[index] = modes.reshape(mode_send.shape[1:])
        if index == 0:
            pl.semaphore_wait(barrier, space_count + data_count - 2)
        mode_copies.append(
            over_space(
                lambda peer, index=index: mode_send.at[index, peer], mode_recv.at[index, space]
            )
        )
        mode_recv[index, space] = mode_send[index, space]

    finish(hidden_loads)
    probe = mxu(tokens(hidden_ref), start_ref[...], NT).astype(bf16)
    finish(normed_loads)
    total = mxu(probe, tokens(normed_ref), TN)
    rank_part = sketch_local.shape[1]
    for peer in range(data_count):
        sketch_local[peer] = total[peer * rank_part : (peer + 1) * rank_part]
    sketch_copies = over_data(lambda peer: sketch_local.at[peer], sketch_recv.at[data])
    sketch_recv[data] = sketch_local[data]

    column = lax.broadcasted_iota(jnp.int32, (BS, group), 1)
    place = lax.broadcasted_iota(jnp.int32, (BS, group), 0)
    repeat = jnp.where(lax.rem(column, BS) == place, 1.0, 0.0).astype(bf16)
    finish(other_loads)
    for source, target in ((inner_ref, inner_wide), (outer_ref, outer_wide)):
        for block in range(2 * NB):
            rows = slice(block * BS, (block + 1) * BS)
            wide = mxu(source[rows, :], repeat)
            target[rows, :] = jnp.where(lax.div(column, BS) == block % 4, wide, 0.0).astype(bf16)

    def wide_weight(ref, part, index):
        first = (part * (NB // 4) + index) * group
        return ref[first : first + group, :]

    for index, lanes in enumerate(groups):
        values = spectrum_ref[:, lanes]
        by_real = mxu(values, wide_weight(inner_wide, 0, index))
        by_imag = mxu(values, wide_weight(inner_wide, 1, index))
        for rows, hidden in (
            (slice(0, half), by_real[:half] - by_imag[half:]),
            (slice(half, 2 * half), by_imag[:half] + by_real[half:]),
        ):
            cdf = 0.5 * (1.0 + lax.erf(hidden * math.sqrt(0.5)))
            density = jnp.exp(-0.5 * hidden * hidden) * (1.0 / math.sqrt(2.0 * math.pi))
            act_ref[rows, lanes] = (hidden * cdf).astype(bf16)
            slope_ref[rows, lanes] = cdf + hidden * density

    arrive(sketch_copies)
    part = sketch_recv[0]
    for peer in range(1, data_count):
        part = part + sketch_recv[peer]
    sketch_part[...] = part
    cross_copies = over_space(lambda peer: sketch_part, sketch_cross.at[space])
    sketch_cross[space] = part

    full = 2 * half
    lane = lax.broadcasted_iota(jnp.int32, (full, KLON), 1)
    row_id = lax.broadcasted_iota(jnp.int32, (full, KLON), 0)
    mode_id = space * mode_local + lax.rem(row_id, mode_local)
    own_cut = jnp.where(lane == mode_id, cutoff_ref[...].astype(f32), 0.0)
    cut = jnp.sum(own_cut, axis=1, keepdims=True)
    row_id = lax.broadcasted_iota(jnp.int32, (full, 1), 0)
    frequency = lax.rem(lax.div(row_id, mode_local), lat_count)
    size = jnp.where(frequency < lat_count // 2, frequency, lat_count - frequency).astype(f32)
    double = jnp.where(space * mode_local + lax.rem(row_id, mode_local) == 0, 1.0, 2.0)
    weight = jnp.where(size < cut, double, 0.0)

    arrive(cross_copies)
    part = sketch_cross[0]
    for peer in range(1, space_count):
        part = part + sketch_cross[peer]
    sketch_full[data] = part
    full_copies = over_data(lambda peer: sketch_full.at[data], sketch_full.at[data])

    lane_block = lax.div(lax.broadcasted_iota(jnp.int32, (BS, group), 1), BS)
    back_copies = []
    core_copies = []
    pair = data + 1 - 2 * core
    for index, lanes in enumerate(groups):
        arrive(mode_copies[index])
        arrived = mode_recv[index].reshape(full, group)
        cot_ref[:, lanes] = (mxu(lat_ref[...], arrived) * weight).astype(bf16)
        values = cot_ref[:, lanes]
        by_real = mxu(values, wide_weight(outer_wide, 0, index), NT)
        by_imag = mxu(values, wide_weight(outer_wide, 1, index), NT)
        real = (by_real[:half] + by_imag[half:]) * slope_ref[:half, lanes]
        imag = (by_real[half:] - by_imag[:half]) * slope_ref[half:, lanes]
        hid_ref[:half, lanes] = real.astype(bf16)
        hid_ref[half:, lanes] = imag.astype(bf16)
        values = hid_ref[:, lanes]
        by_real = mxu(values, wide_weight(inner_wide, 0, index), NT)
        by_imag = mxu(values, wide_weight(inner_wide, 1, index), NT)
        xg_ref[:half, lanes] = (by_real[:half] + by_imag[half:]).astype(bf16)
        xg_ref[half:, lanes] = (by_real[half:] - by_imag[:half]).astype(bf16)
        back = mxu(back_ref[...], xg_ref[:, lanes]).astype(bf16)
        back_send[index] = back.reshape(back_send.shape[1:])
        back_copies += over_space(
            lambda peer, index=index: back_send.at[index, peer], back_recv.at[index, space]
        )
        back_recv[index, space] = back_send[index, space]

        for first, left, right in ((0, spectrum_ref, hid_ref), (1, act_ref, cot_ref)):
            values = left[:, lanes]
            turned = jnp.concatenate([right[half:, lanes], -right[:half, lanes]], axis=0)
            parts = []
            for other in (right[:, lanes], turned):
                product = mxu(values, other, TN)
                compact = jnp.zeros((BS, group), f32)
                for block in range(4):
                    compact = jnp.where(
                        lane_block == block, product[block * BS : (block + 1) * BS], compact
                    )
                parts.append(compact)
            rows = slice(first * BS, (first + 1) * BS)
            low = lane_block < 2
            wide_send[0, index, rows, :] = jnp.where(
                low, parts[0], pltpu.roll(parts[1], 2 * BS, 1)
            ).astype(bf16)
            wide_send[1, index, rows, :] = jnp.where(
                low, pltpu.roll(parts[0], 2 * BS, 1), parts[1]
            ).astype(bf16)
        core_copies.append(
            push(wide_send.at[1 - core, index], wide_recv.at[index], {"dp": pair})
        )

    arrive(core_copies)
    mine = wide_send[core].astype(f32) + wide_recv[...].astype(f32)
    wide_recv[...] = mine.astype(bf16)
    chip_copy = push(wide_recv.at[1 - chip], half_recv, {"dp": lax.rem(data + 2, data_count)})

    arrive(full_copies)
    sketch = sketch_full[...].reshape(data_count * rank_part, D)
    gram = lax.dot_general(
        sketch, sketch, NT, precision=HIGHEST, preferred_element_type=f32
    )
    rank = sketch.shape[0]
    rank_row = lax.broadcasted_iota(jnp.int32, (rank, 1), 0)
    for step in range(rank - 1):
        pivot = gram[step : step + 1, step : step + 1]
        ratio = jnp.where(rank_row > step, gram[:, step : step + 1] / pivot, 0.0)
        sketch = sketch - ratio * sketch[step : step + 1, :]
        gram = gram - ratio * gram[step : step + 1, :]
    eye = lax.broadcasted_iota(jnp.int32, (rank, rank), 0) == lax.broadcasted_iota(
        jnp.int32, (rank, rank), 1
    )
    diagonal = jnp.sum(jnp.where(eye, gram, 0.0), axis=1, keepdims=True)
    scale = 1.0 / jnp.sqrt(diagonal)
    left_factor = sketch * scale
    left_out[...] = left_factor
    left_round = left_factor.astype(bf16)

    chip_copy.wait_recv()
    mine = wide_recv[chip].astype(f32) + half_recv[...].astype(f32)
    quarter_send[...] = mine.astype(bf16).reshape(quarter_send.shape)
    quarter_copies = over_space(lambda peer: quarter_send.at[peer], quarter_recv.at[space])
    quarter_recv[space] = quarter_send[space]

    mixed = mxu(left_round, tokens(normed_ref), NT).astype(bf16)
    total = mxu(mixed, tokens(hidden_ref)).astype(bf16)
    share = FF // (space_count * data_count)
    for owner in range(space_count * data_count):
        first = owner * share // 128 * 128
        right_send[owner % data_count, owner // data_count] = total[:, first : first + 256]
    right_copies = over_data(lambda peer: right_send.at[peer], right_recv.at[data])
    right_recv[data] = right_send[data]

    arrive(right_copies)
    part = right_recv[0].astype(f32)
    for peer in range(1, data_count):
        part = part + right_recv[peer].astype(f32)
    right_part[...] = part.astype(bf16)
    last_copies = over_space(lambda peer: right_part.at[peer], right_cross.at[space])
    right_cross[space] = right_part[space]

    arrive(quarter_copies)
    part = quarter_recv[0].astype(f32)
    for peer in range(1, space_count):
        part = part + quarter_recv[peer].astype(f32)
    piece_all[space] = part.astype(bf16)
    piece_copies = over_space(lambda peer: piece_all.at[space], piece_all.at[space])

    arrive(back_copies)
    grid_view = grid_out.reshape(grid_out.shape[0], token_count, 128)
    stores = []
    grid_tokens_again = tokens(grid_ref)
    for index, lanes in enumerate(groups):
        arrived = back_recv[index].reshape(full, group)
        result = grid_tokens_again[:, lanes].astype(f32) + mxu(spread_ref[...], arrived)
        result = result.astype(bf16)
        for tile in range(group // 128):
            place = index * (group // 128) + tile
            grid_view[place] = result[:, tile * 128 : (tile + 1) * 128]
            stores.append(
                load(
                    grid_out.at[place],
                    grid_hbm_out.at[:, :, place * 128 : (place + 1) * 128],
                )
            )

    arrive(last_copies)
    part = right_cross[0].astype(f32)
    for peer in range(1, space_count):
        part = part + right_cross[peer].astype(f32)
    part = jnp.where(core == 1, pltpu.roll(part, 192, 1), part)
    right_out[...] = part[:, : 2 * BS] * (1.0 / math.sqrt(data_count * lat_count * LON))

    arrive(piece_copies)
    result = piece_all[...].reshape(2 * BS, group).astype(f32)
    result = result * (1.0 / math.sqrt(data_count * lat_count * KLON))
    for place in range(4):
        turned = result if place == 0 else pltpu.roll(result, group - place * BS, 1)
        inner_out[place // 2, place % 2] = turned[:BS, :BS]
        outer_out[place // 2, place % 2] = turned[BS:, :BS]
    finish(stores)
    for copy in pending:
        copy.wait_send()


def fused_body(
    grad_mid, spectrum, filter_inner, filter_outer, cutoff, normed_mid, hidden_grad, power_start
):
    space_count = lax.axis_size("space")
    data_count = lax.axis_size("dp")
    row_count = grad_mid.shape[1]
    mode_local = KLON // space_count
    modes = 2 * row_count * space_count * mode_local
    rank = power_start.shape[1]
    bf16, f32 = jnp.bfloat16, jnp.float32
    lon_table, spread, lat_table, back_table = fused_tables(space_count, row_count)
    vmem = pl.BlockSpec(memory_space=pltpu.VMEM)
    anywhere = pl.BlockSpec(memory_space=pl.ANY)
    slab = (NB // 4, space_count, row_count * 2 * mode_local, 4 * BS)
    copies = 8 * (space_count - 1) + 3 * (data_count - 1) + 3
    grid_shape = (D // 128, LON, row_count, 128)
    grid_out, inner_out, outer_out, left_out, right_out = pl.pallas_call(
        fused_kernel,
        out_shape=(
            jax.ShapeDtypeStruct((LON, row_count, D), bf16),
            jax.ShapeDtypeStruct((2, 2, BS, BS), f32),
            jax.ShapeDtypeStruct((2, 2, BS, BS), f32),
            jax.ShapeDtypeStruct((rank, D), f32),
            jax.ShapeDtypeStruct((rank, 2 * BS), f32),
        ),
        in_specs=[anywhere] * 4 + [vmem] + [anywhere] * 7,
        out_specs=(anywhere,) + (vmem,) * 4,
        scratch_shapes=[
            pltpu.VMEM((modes, LON * row_count), bf16),
            pltpu.VMEM((LON * row_count, modes), bf16),
            pltpu.VMEM((modes, modes), bf16),
            pltpu.VMEM((modes, modes), bf16),
            pltpu.VMEM(grid_shape, bf16),
            pltpu.VMEM(grid_shape, bf16),
            pltpu.VMEM((modes, D), bf16),
            pltpu.VMEM((2 * NB * BS, BS), bf16),
            pltpu.VMEM((2 * NB * BS, BS), bf16),
            pltpu.VMEM(grid_shape, bf16),
            pltpu.VMEM((FF // 128, LON, row_count, 128), bf16),
            pltpu.VMEM((rank, FF), bf16),
            pltpu.VMEM((2 * NB * BS, 4 * BS), bf16),
            pltpu.VMEM((2 * NB * BS, 4 * BS), bf16),
            pltpu.VMEM((modes, D), bf16),
            pltpu.VMEM((modes, D), f32),
            pltpu.VMEM((modes, D), bf16),
            pltpu.VMEM((modes, D), bf16),
            pltpu.VMEM((modes, D), bf16),
            pltpu.VMEM(slab, bf16),
            pltpu.VMEM(slab, bf16),
            pltpu.VMEM(slab, bf16),
            pltpu.VMEM(slab, bf16),
            pltpu.VMEM((data_count, rank // data_count, D), f32),
            pltpu.VMEM((data_count, rank // data_count, D), f32),
            pltpu.VMEM((rank // data_count, D), f32),
            pltpu.VMEM((space_count, rank // data_count, D), f32),
            pltpu.VMEM((data_count, rank // data_count, D), f32),
            pltpu.VMEM((data_count, space_count, rank, 256), bf16),
            pltpu.VMEM((data_count, space_count, rank, 256), bf16),
            pltpu.VMEM((space_count, rank, 256), bf16),
            pltpu.VMEM((space_count, rank, 256), bf16),
            pltpu.VMEM((2, 2, 2 * BS, 4 * BS), bf16),
            pltpu.VMEM((2, 2 * BS, 4 * BS), bf16),
            pltpu.VMEM((2 * BS, 4 * BS), bf16),
            pltpu.VMEM((space_count, 2 * BS // space_count, 4 * BS), bf16),
            pltpu.VMEM((space_count, 2 * BS // space_count, 4 * BS), bf16),
            pltpu.VMEM((space_count, 2 * BS // space_count, 4 * BS), bf16),
            pltpu.SemaphoreType.DMA((3 * (D // 128) + FF // 128 + 8,)),
            pltpu.SemaphoreType.DMA((copies,)),
            pltpu.SemaphoreType.DMA((copies,)),
        ],
        compiler_params=pltpu.CompilerParams(
            collective_id=0, has_side_effects=True, vmem_limit_bytes=60 * 1024 * 1024
        ),
        name="fused_filter_sketch",
    )(
        grad_mid.transpose(0, 2, 1, 3).reshape(LON, row_count, D),
        spectrum.reshape(modes, D),
        filter_inner.reshape(2 * NB * BS, BS),
        filter_outer.reshape(2 * NB * BS, BS),
        cutoff.reshape(1, KLON),
        normed_mid.transpose(0, 2, 1, 3).reshape(LON, row_count, D),
        hidden_grad.transpose(0, 2, 1, 3).reshape(LON, row_count, FF),
        power_start.T,
        lon_table,
        spread,
        lat_table,
        back_table,
    )
    grid = grid_out.reshape(1, LON, row_count, D).transpose(0, 2, 1, 3)
    return (grid, inner_out, outer_out, left_out.T, right_out.T)


def solution(mesh):
    in_specs = (
        P(("groups", "dp"), "space", None, None),
        P(None, ("groups", "dp"), None, "space", None),
        P(),
        P(),
        P(),
        P(("groups", "dp"), "space", None, None),
        P(("groups", "dp"), "space", None, None),
        P(),
    )
    out_specs = (
        P(("groups", "dp"), "space", None, None),
        P("groups", "dp", None, None),
        P("groups", "dp", None, None),
        P("groups", None),
        P(("groups", "space", "dp"), None),
    )
    fits = mesh.shape["space"] == 4 and mesh.shape["dp"] == 4
    chosen = fused_body if fits else body
    return jax.shard_map(chosen, mesh=mesh, in_specs=in_specs, out_specs=out_specs, check_vma=False)
```

```python
import math

import jax
import jax.numpy as jnp
import numpy as np
from jax import lax
from jax.experimental import pallas as pl
from jax.experimental.pallas import tpu as pltpu
from jax.sharding import PartitionSpec as P

D = 768
NB = 8
BS = 96
FF = 3072
LON = 180
KLON = 64


HIGHEST = lax.Precision.HIGHEST


def angle_table(left_count, right_count, length):
    left_index = jnp.arange(left_count, dtype=jnp.int32)[:, None]
    right_index = jnp.arange(right_count, dtype=jnp.int32)[None, :]
    angles = (left_index * right_index % length).astype(jnp.float32) * (2.0 * math.pi / length)
    return (jnp.cos(angles), jnp.sin(angles))


def lon_forward(grid_values, cosine_table, sine_table, factor):
    real_part = jnp.einsum("srlc,kl->srkc", grid_values, cosine_table) * factor
    imag_part = -jnp.einsum("srlc,kl->srkc", grid_values, sine_table) * factor
    return jnp.stack([real_part, imag_part])


def lat_forward(complex_pair, cosine_table, sine_table):
    real_part = jnp.einsum(
        "jt,stkc->sjkc", cosine_table, complex_pair[0]
    ) + jnp.einsum("jt,stkc->sjkc", sine_table, complex_pair[1])
    imag_part = jnp.einsum(
        "jt,stkc->sjkc", cosine_table, complex_pair[1]
    ) - jnp.einsum("jt,stkc->sjkc", sine_table, complex_pair[0])
    return jnp.stack([real_part, imag_part])


def lat_adjoint(complex_pair, cosine_table, sine_table):
    real_part = jnp.einsum(
        "jt,sjkc->stkc", cosine_table, complex_pair[0]
    ) - jnp.einsum("jt,sjkc->stkc", sine_table, complex_pair[1])
    imag_part = jnp.einsum(
        "jt,sjkc->stkc", sine_table, complex_pair[0]
    ) + jnp.einsum("jt,sjkc->stkc", cosine_table, complex_pair[1])
    return jnp.stack([real_part, imag_part])


def lon_adjoint(complex_pair, cosine_table, sine_table, factor):
    summed = jnp.einsum(
        "srkc,kl->srlc", complex_pair[0], cosine_table
    ) - jnp.einsum("srkc,kl->srlc", complex_pair[1], sine_table)
    return summed * factor


def mode_weight(lat_count, first_mode, mode_count, cut_local):
    frequency = jnp.arange(lat_count, dtype=jnp.int32)
    signed = jnp.where(frequency < lat_count // 2, frequency, frequency - lat_count)
    mode_index = first_mode + jnp.arange(mode_count, dtype=jnp.int32)
    double = jnp.where(mode_index == 0, 1.0, 2.0)
    retained = jnp.abs(signed)[:, None] < cut_local[None, :]
    return jnp.where(retained, double[None, :], 0.0).astype(jnp.float32)


def complex_product(real_part, imag_part, weights):
    out_real = jnp.einsum("rbi,bio->rbo", real_part, weights[0]) - jnp.einsum(
        "rbi,bio->rbo", imag_part, weights[1]
    )
    out_imag = jnp.einsum("rbi,bio->rbo", real_part, weights[1]) + jnp.einsum(
        "rbi,bio->rbo", imag_part, weights[0]
    )
    return (out_real, out_imag)


def spectral_filter(real_part, imag_part, inner_weights, outer_weights):
    hidden_real, hidden_imag = complex_product(real_part, imag_part, inner_weights)
    return complex_product(
        jax.nn.gelu(hidden_real, approximate=False),
        jax.nn.gelu(hidden_imag, approximate=False),
        outer_weights,
    )


def filter_backward(spectrum_pair, cotangent, inner_weights, outer_weights):

    def shaped(values):
        return values.reshape(-1, NB, BS)

    outputs, pullback = jax.vjp(
        spectral_filter,
        shaped(spectrum_pair[0]),
        shaped(spectrum_pair[1]),
        inner_weights,
        outer_weights,
    )
    gradients = pullback((shaped(cotangent[0]), shaped(cotangent[1])))
    block_shape = spectrum_pair.shape[1:]
    mode_grad = jnp.stack([gradients[0].reshape(block_shape), gradients[1].reshape(block_shape)])
    return (mode_grad, gradients[2], gradients[3])


def orthonormal(sketch):
    gram_matrix = jnp.dot(sketch.T, sketch, precision=HIGHEST)
    cholesky_factor = jnp.linalg.cholesky(gram_matrix)
    return lax.linalg.triangular_solve(
        cholesky_factor, sketch, left_side=False, lower=True, transpose_a=True
    )


def body(
    grad_mid, spectrum, filter_inner, filter_outer, cutoff, normed_mid, hidden_grad, power_start
):
    space_count = lax.axis_size("space")
    data_count = lax.axis_size("dp")
    sample_count = grad_mid.shape[0]
    lat_count = grad_mid.shape[1] * space_count
    mode_local = KLON // space_count
    factor = 1.0 / math.sqrt(lat_count * LON)
    tokens_mid = normed_mid.reshape(-1, D)
    tokens_grad = hidden_grad.reshape(-1, FF)
    probe = jnp.dot(tokens_grad, power_start, preferred_element_type=jnp.float32).astype(
        jnp.bfloat16
    )
    sketch_local = jnp.dot(tokens_mid.T, probe, preferred_element_type=jnp.float32)
    sketch = lax.psum(sketch_local, ("space", "dp"))
    grad_float = grad_mid.astype(jnp.float32)
    lon_cos, lon_sin = angle_table(KLON, LON, LON)
    lat_cos, lat_sin = angle_table(lat_count, lat_count, lat_count)
    row_spectra = lon_forward(grad_float, lon_cos, lon_sin, factor)
    mode_values = lat_forward(
        lax.all_to_all(
            row_spectra.astype(jnp.bfloat16), "space", split_axis=3, concat_axis=2, tiled=True
        ).astype(jnp.float32),
        lat_cos,
        lat_sin,
    )
    first_mode = lax.axis_index("space") * mode_local
    cut_local = lax.dynamic_slice_in_dim(cutoff, first_mode, mode_local)
    weight = mode_weight(lat_count, first_mode, mode_local, cut_local)
    cotangent = mode_values * weight[None, None, :, :, None]
    mode_grad, inner_grad, outer_grad = filter_backward(
        spectrum.astype(jnp.float32),
        cotangent,
        filter_inner.astype(jnp.float32),
        filter_outer.astype(jnp.float32),
    )
    back = lat_adjoint(mode_grad, lat_cos, lat_sin)
    row_back = lax.all_to_all(
        back.astype(jnp.bfloat16), "space", split_axis=2, concat_axis=3, tiled=True
    ).astype(jnp.float32)
    spectral_grad = lon_adjoint(row_back, lon_cos, lon_sin, factor)
    grad_input = (grad_float + spectral_grad).astype(jnp.bfloat16)
    inner_grad, outer_grad = (
        lax.psum_scatter(
            inner_grad.astype(jnp.bfloat16), "dp", scatter_dimension=1, tiled=True
        ).astype(jnp.float32),
        lax.psum_scatter(
            outer_grad.astype(jnp.bfloat16), "dp", scatter_dimension=1, tiled=True
        ).astype(jnp.float32),
    )
    inner_grad, outer_grad = (
        lax.psum(inner_grad.astype(jnp.bfloat16), "space").astype(jnp.float32),
        lax.psum(outer_grad.astype(jnp.bfloat16), "space").astype(jnp.float32),
    )
    grad_factor = 1.0 / math.sqrt(sample_count * data_count * lat_count * KLON)
    left_factor = orthonormal(sketch)
    left_round = left_factor.astype(jnp.bfloat16)
    mixed = jnp.dot(tokens_mid, left_round, preferred_element_type=jnp.float32).astype(jnp.bfloat16)
    right_sum = lax.psum_scatter(
        jnp.dot(tokens_grad.T, mixed, preferred_element_type=jnp.float32),
        ("space", "dp"),
        scatter_dimension=0,
        tiled=True,
    )
    right_factor = right_sum * (1.0 / math.sqrt(sample_count * data_count * lat_count * LON))
    return (
        grad_input,
        inner_grad * grad_factor,
        outer_grad * grad_factor,
        left_factor,
        right_factor,
    )


def fused_tables(space_count, row_count):
    lat_count = space_count * row_count
    mode_local = KLON // space_count
    factor = 1.0 / math.sqrt(lat_count * LON)
    angle = (np.outer(np.arange(KLON), np.arange(LON)) % LON) * (2.0 * math.pi / LON)
    pair = np.stack([np.cos(angle), -np.sin(angle)]) * factor
    lon_table = (
        pair.reshape(2, space_count, mode_local, LON)
        .transpose(1, 0, 2, 3)
        .reshape(2 * KLON, LON)
    )
    spread = np.zeros((LON, row_count, space_count, row_count, 2 * mode_local))
    for row in range(row_count):
        spread[:, row, :, row, :] = lon_table.T.reshape(LON, space_count, 2 * mode_local)
    spread = spread.reshape(LON * row_count, space_count * row_count * 2 * mode_local)
    angle = (np.outer(np.arange(lat_count), np.arange(lat_count)) % lat_count) * (
        2.0 * math.pi / lat_count
    )
    cosine, sine = np.cos(angle), np.sin(angle)
    mix = np.stack([np.stack([cosine, sine], -1), np.stack([-sine, cosine], -1)])
    lat_table = np.einsum("ojti,kl->ojktil", mix, np.eye(mode_local)).reshape(
        2 * lat_count * mode_local, 2 * lat_count * mode_local
    )
    as_bf16 = lambda values: jnp.asarray(values.astype(np.float32), jnp.bfloat16)
    return as_bf16(spread.T.copy()), as_bf16(spread), as_bf16(lat_table), as_bf16(lat_table.T.copy())


NN = (((1,), (0,)), ((), ()))
NT = (((1,), (1,)), ((), ()))
TN = (((0,), (0,)), ((), ()))


def mxu(left, right, dims=NN):
    return lax.dot_general(left, right, dims, preferred_element_type=jnp.float32)


def fused_kernel(
    grid_hbm,
    spectrum_hbm,
    inner_hbm,
    outer_hbm,
    cutoff_ref,
    normed_hbm,
    hidden_hbm,
    start_hbm,
    lon_hbm,
    spread_hbm,
    lat_hbm,
    back_hbm,
    grid_hbm_out,
    inner_out,
    outer_out,
    left_out,
    right_out,
    lon_ref,
    spread_ref,
    lat_ref,
    back_ref,
    grid_out,
    grid_ref,
    spectrum_ref,
    inner_ref,
    outer_ref,
    normed_ref,
    hidden_ref,
    start_ref,
    inner_wide,
    outer_wide,
    act_ref,
    slope_ref,
    cot_ref,
    hid_ref,
    xg_ref,
    mode_send,
    mode_recv,
    back_send,
    back_recv,
    sketch_local,
    sketch_recv,
    sketch_part,
    sketch_cross,
    sketch_full,
    right_send,
    right_recv,
    right_part,
    right_cross,
    wide_send,
    wide_recv,
    half_recv,
    quarter_send,
    quarter_recv,
    piece_all,
    local_sem,
    send_sem,
    recv_sem,
):
    bf16, f32 = jnp.bfloat16, jnp.float32
    space, data = lax.axis_index("space"), lax.axis_index("dp")
    space_count, data_count = mode_send.shape[1], sketch_recv.shape[0]
    core, chip = lax.rem(data, 2), lax.div(data, 2)
    row_count = grid_ref.shape[2]
    token_count = grid_ref.shape[1] * row_count
    half = spectrum_ref.shape[0] // 2
    mode_local = KLON // space_count
    lat_count = row_count * space_count

    used = 0

    def load(source, target):
        nonlocal used
        copy = pltpu.make_async_copy(source, target, local_sem.at[used])
        copy.start()
        used += 1
        return copy

    def load_tokens(source, target):
        return [
            load(source.at[:, :, index * 128 : (index + 1) * 128], target.at[index])
            for index in range(target.shape[0])
        ]

    def finish(copies):
        for copy in copies:
            copy.wait()

    def tokens(ref):
        view = ref.reshape(ref.shape[0], token_count, 128)
        return jnp.concatenate([view[index] for index in range(ref.shape[0])], axis=1)

    grid_loads = load_tokens(grid_hbm, grid_ref) + [load(lon_hbm, lon_ref)]
    hidden_loads = load_tokens(hidden_hbm, hidden_ref) + [load(start_hbm, start_ref)]
    normed_loads = load_tokens(normed_hbm, normed_ref)
    other_loads = [
        load(source, target)
        for source, target in (
            (inner_hbm, inner_ref),
            (spectrum_hbm, spectrum_ref),
            (outer_hbm, outer_ref),
            (lat_hbm, lat_ref),
            (back_hbm, back_ref),
            (spread_hbm, spread_ref),
        )
    ]

    barrier = pltpu.get_barrier_semaphore()
    for step in range(1, space_count):
        pl.semaphore_signal(
            barrier,
            inc=1,
            device_id={"space": lax.rem(space + step, space_count)},
            device_id_type=pl.DeviceIdType.MESH,
        )
    for step in range(1, data_count):
        pl.semaphore_signal(
            barrier,
            inc=1,
            device_id={"dp": lax.rem(data + step, data_count)},
            device_id_type=pl.DeviceIdType.MESH,
        )

    pending = []

    def push(source, target, device):
        index = len(pending)
        copy = pltpu.make_async_remote_copy(
            src_ref=source,
            dst_ref=target,
            send_sem=send_sem.at[index],
            recv_sem=recv_sem.at[index],
            device_id=device,
            device_id_type=pl.DeviceIdType.MESH,
        )
        copy.start()
        pending.append(copy)
        return copy

    def over_space(source, target):
        copies = []
        for step in range(1, space_count):
            peer = lax.rem(space + step, space_count)
            copies.append(push(source(peer), target, {"space": peer}))
        return copies

    def over_data(source, target):
        copies = []
        for step in range(1, data_count):
            peer = lax.rem(data + step, data_count)
            copies.append(push(source(peer), target, {"dp": peer}))
        return copies

    def arrive(copies):
        for copy in copies:
            copy.wait_recv()

    group = 4 * BS
    groups = [slice(index * group, (index + 1) * group) for index in range(NB // 4)]
    finish(grid_loads)
    grid_tokens = tokens(grid_ref)
    mode_copies = []
    for index, lanes in enumerate(groups):
        modes = mxu(lon_ref[...], grid_tokens[:, lanes]).astype(bf16)
        mode_send[index] = modes.reshape(mode_send.shape[1:])
        if index == 0:
            pl.semaphore_wait(barrier, space_count + data_count - 2)
        mode_copies.append(
            over_space(
                lambda peer, index=index: mode_send.at[index, peer], mode_recv.at[index, space]
            )
        )
        mode_recv[index, space] = mode_send[index, space]

    finish(hidden_loads)
    probe = mxu(tokens(hidden_ref), start_ref[...], NT).astype(bf16)
    finish(normed_loads)
    total = mxu(probe, tokens(normed_ref), TN)
    rank_part = sketch_local.shape[1]
    for peer in range(data_count):
        sketch_local[peer] = total[peer * rank_part : (peer + 1) * rank_part]
    sketch_copies = over_data(lambda peer: sketch_local.at[peer], sketch_recv.at[data])
    sketch_recv[data] = sketch_local[data]

    column = lax.broadcasted_iota(jnp.int32, (BS, group), 1)
    place = lax.broadcasted_iota(jnp.int32, (BS, group), 0)
    repeat = jnp.where(lax.rem(column, BS) == place, 1.0, 0.0).astype(bf16)
    finish(other_loads)
    for source, target in ((inner_ref, inner_wide), (outer_ref, outer_wide)):
        for block in range(2 * NB):
            rows = slice(block * BS, (block + 1) * BS)
            wide = mxu(source[rows, :], repeat)
            target[rows, :] = jnp.where(lax.div(column, BS) == block % 4, wide, 0.0).astype(bf16)

    def wide_weight(ref, part, index):
        first = (part * (NB // 4) + index) * group
        return ref[first : first + group, :]

    for index, lanes in enumerate(groups):
        values = spectrum_ref[:, lanes]
        by_real = mxu(values, wide_weight(inner_wide, 0, index))
        by_imag = mxu(values, wide_weight(inner_wide, 1, index))
        for rows, hidden in (
            (slice(0, half), by_real[:half] - by_imag[half:]),
            (slice(half, 2 * half), by_imag[:half] + by_real[half:]),
        ):
            cdf = 0.5 * (1.0 + lax.erf(hidden * math.sqrt(0.5)))
            density = jnp.exp(-0.5 * hidden * hidden) * (1.0 / math.sqrt(2.0 * math.pi))
            act_ref[rows, lanes] = (hidden * cdf).astype(bf16)
            slope_ref[rows, lanes] = cdf + hidden * density

    arrive(sketch_copies)
    part = sketch_recv[0]
    for peer in range(1, data_count):
        part = part + sketch_recv[peer]
    sketch_part[...] = part
    cross_copies = over_space(lambda peer: sketch_part, sketch_cross.at[space])
    sketch_cross[space] = part

    full = 2 * half
    lane = lax.broadcasted_iota(jnp.int32, (full, KLON), 1)
    row_id = lax.broadcasted_iota(jnp.int32, (full, KLON), 0)
    mode_id = space * mode_local + lax.rem(row_id, mode_local)
    own_cut = jnp.where(lane == mode_id, cutoff_ref[...].astype(f32), 0.0)
    cut = jnp.sum(own_cut, axis=1, keepdims=True)
    row_id = lax.broadcasted_iota(jnp.int32, (full, 1), 0)
    frequency = lax.rem(lax.div(row_id, mode_local), lat_count)
    size = jnp.where(frequency < lat_count // 2, frequency, lat_count - frequency).astype(f32)
    double = jnp.where(space * mode_local + lax.rem(row_id, mode_local) == 0, 1.0, 2.0)
    weight = jnp.where(size < cut, double, 0.0)

    arrive(cross_copies)
    part = sketch_cross[0]
    for peer in range(1, space_count):
        part = part + sketch_cross[peer]
    sketch_full[data] = part
    full_copies = over_data(lambda peer: sketch_full.at[data], sketch_full.at[data])

    lane_block = lax.div(lax.broadcasted_iota(jnp.int32, (BS, group), 1), BS)
    back_copies = []
    core_copies = []
    pair = data + 1 - 2 * core
    for index, lanes in enumerate(groups):
        arrive(mode_copies[index])
        arrived = mode_recv[index].reshape(full, group)
        cot_ref[:, lanes] = (mxu(lat_ref[...], arrived) * weight).astype(bf16)
        values = cot_ref[:, lanes]
        by_real = mxu(values, wide_weight(outer_wide, 0, index), NT)
        by_imag = mxu(values, wide_weight(outer_wide, 1, index), NT)
        real = (by_real[:half] + by_imag[half:]) * slope_ref[:half, lanes]
        imag = (by_real[half:] - by_imag[:half]) * slope_ref[half:, lanes]
        hid_ref[:half, lanes] = real.astype(bf16)
        hid_ref[half:, lanes] = imag.astype(bf16)
        values = hid_ref[:, lanes]
        by_real = mxu(values, wide_weight(inner_wide, 0, index), NT)
        by_imag = mxu(values, wide_weight(inner_wide, 1, index), NT)
        xg_ref[:half, lanes] = (by_real[:half] + by_imag[half:]).astype(bf16)
        xg_ref[half:, lanes] = (by_real[half:] - by_imag[:half]).astype(bf16)
        back = mxu(back_ref[...], xg_ref[:, lanes]).astype(bf16)
        back_send[index] = back.reshape(back_send.shape[1:])
        back_copies += over_space(
            lambda peer, index=index: back_send.at[index, peer], back_recv.at[index, space]
        )
        back_recv[index, space] = back_send[index, space]

        for first, left, right in ((0, spectrum_ref, hid_ref), (1, act_ref, cot_ref)):
            values = left[:, lanes]
            turned = jnp.concatenate([right[half:, lanes], -right[:half, lanes]], axis=0)
            parts = []
            for other in (right[:, lanes], turned):
                product = mxu(values, other, TN)
                compact = jnp.zeros((BS, group), f32)
                for block in range(4):
                    compact = jnp.where(
                        lane_block == block, product[block * BS : (block + 1) * BS], compact
                    )
                parts.append(compact)
            rows = slice(first * BS, (first + 1) * BS)
            low = lane_block < 2
            wide_send[0, index, rows, :] = jnp.where(
                low, parts[0], pltpu.roll(parts[1], 2 * BS, 1)
            ).astype(bf16)
            wide_send[1, index, rows, :] = jnp.where(
                low, pltpu.roll(parts[0], 2 * BS, 1), parts[1]
            ).astype(bf16)
        core_copies.append(
            push(wide_send.at[1 - core, index], wide_recv.at[index], {"dp": pair})
        )

    arrive(core_copies)
    mine = wide_send[core].astype(f32) + wide_recv[...].astype(f32)
    wide_recv[...] = mine.astype(bf16)
    chip_copy = push(wide_recv.at[1 - chip], half_recv, {"dp": lax.rem(data + 2, data_count)})

    arrive(full_copies)
    sketch = sketch_full[...].reshape(data_count * rank_part, D)
    gram = lax.dot_general(
        sketch, sketch, NT, precision=HIGHEST, preferred_element_type=f32
    )
    rank = sketch.shape[0]
    rank_row = lax.broadcasted_iota(jnp.int32, (rank, 1), 0)
    for step in range(rank - 1):
        pivot = gram[step : step + 1, step : step + 1]
        ratio = jnp.where(rank_row > step, gram[:, step : step + 1] / pivot, 0.0)
        sketch = sketch - ratio * sketch[step : step + 1, :]
        gram = gram - ratio * gram[step : step + 1, :]
    eye = lax.broadcasted_iota(jnp.int32, (rank, rank), 0) == lax.broadcasted_iota(
        jnp.int32, (rank, rank), 1
    )
    diagonal = jnp.sum(jnp.where(eye, gram, 0.0), axis=1, keepdims=True)
    scale = 1.0 / jnp.sqrt(diagonal)
    left_factor = sketch * scale
    left_out[...] = left_factor
    left_round = left_factor.astype(bf16)

    chip_copy.wait_recv()
    mine = wide_recv[chip].astype(f32) + half_recv[...].astype(f32)
    quarter_send[...] = mine.astype(bf16).reshape(quarter_send.shape)
    quarter_copies = over_space(lambda peer: quarter_send.at[peer], quarter_recv.at[space])
    quarter_recv[space] = quarter_send[space]

    mixed = mxu(left_round, tokens(normed_ref), NT).astype(bf16)
    total = mxu(mixed, tokens(hidden_ref)).astype(bf16)
    share = FF // (space_count * data_count)
    for owner in range(space_count * data_count):
        first = owner * share // 128 * 128
        right_send[owner % data_count, owner // data_count] = total[:, first : first + 256]
    right_copies = over_data(lambda peer: right_send.at[peer], right_recv.at[data])
    right_recv[data] = right_send[data]

    arrive(right_copies)
    part = right_recv[0].astype(f32)
    for peer in range(1, data_count):
        part = part + right_recv[peer].astype(f32)
    right_part[...] = part.astype(bf16)
    last_copies = over_space(lambda peer: right_part.at[peer], right_cross.at[space])
    right_cross[space] = right_part[space]

    arrive(quarter_copies)
    part = quarter_recv[0].astype(f32)
    for peer in range(1, space_count):
        part = part + quarter_recv[peer].astype(f32)
    piece_all[space] = part.astype(bf16)
    piece_copies = over_space(lambda peer: piece_all.at[space], piece_all.at[space])

    arrive(back_copies)
    grid_view = grid_out.reshape(grid_out.shape[0], token_count, 128)
    stores = []
    grid_tokens_again = tokens(grid_ref)
    for index, lanes in enumerate(groups):
        arrived = back_recv[index].reshape(full, group)
        result = grid_tokens_again[:, lanes].astype(f32) + mxu(spread_ref[...], arrived)
        result = result.astype(bf16)
        for tile in range(group // 128):
            place = index * (group // 128) + tile
            grid_view[place] = result[:, tile * 128 : (tile + 1) * 128]
            stores.append(
                load(
                    grid_out.at[place],
                    grid_hbm_out.at[:, :, place * 128 : (place + 1) * 128],
                )
            )

    arrive(last_copies)
    part = right_cross[0].astype(f32)
    for peer in range(1, space_count):
        part = part + right_cross[peer].astype(f32)
    part = jnp.where(core == 1, pltpu.roll(part, 192, 1), part)
    right_out[...] = part[:, : 2 * BS] * (1.0 / math.sqrt(data_count * lat_count * LON))

    arrive(piece_copies)
    result = piece_all[...].reshape(2 * BS, group).astype(f32)
    result = result * (1.0 / math.sqrt(data_count * lat_count * KLON))
    for place in range(4):
        turned = result if place == 0 else pltpu.roll(result, group - place * BS, 1)
        inner_out[place // 2, place % 2] = turned[:BS, :BS]
        outer_out[place // 2, place % 2] = turned[BS:, :BS]
    finish(stores)
    for copy in pending:
        copy.wait_send()


def fused_body(
    grad_mid, spectrum, filter_inner, filter_outer, cutoff, normed_mid, hidden_grad, power_start
):
    space_count = lax.axis_size("space")
    data_count = lax.axis_size("dp")
    row_count = grad_mid.shape[1]
    mode_local = KLON // space_count
    modes = 2 * row_count * space_count * mode_local
    rank = power_start.shape[1]
    bf16, f32 = jnp.bfloat16, jnp.float32
    lon_table, spread, lat_table, back_table = fused_tables(space_count, row_count)
    vmem = pl.BlockSpec(memory_space=pltpu.VMEM)
    anywhere = pl.BlockSpec(memory_space=pl.ANY)
    held = pl.BlockSpec(memory_space=pltpu.HBM)
    slab = (NB // 4, space_count, row_count * 2 * mode_local, 4 * BS)
    copies = 8 * (space_count - 1) + 3 * (data_count - 1) + 3
    grid_shape = (D // 128, LON, row_count, 128)
    grid_out, inner_out, outer_out, left_out, right_out = pl.pallas_call(
        fused_kernel,
        out_shape=(
            jax.ShapeDtypeStruct((LON, row_count, D), bf16),
            jax.ShapeDtypeStruct((2, 2, BS, BS), f32),
            jax.ShapeDtypeStruct((2, 2, BS, BS), f32),
            jax.ShapeDtypeStruct((rank, D), f32),
            jax.ShapeDtypeStruct((rank, 2 * BS), f32),
        ),
        in_specs=[held] * 4 + [vmem] + [held] * 7,
        out_specs=(anywhere,) + (vmem,) * 4,
        scratch_shapes=[
            pltpu.VMEM((modes, LON * row_count), bf16),
            pltpu.VMEM((LON * row_count, modes), bf16),
            pltpu.VMEM((modes, modes), bf16),
            pltpu.VMEM((modes, modes), bf16),
            pltpu.VMEM(grid_shape, bf16),
            pltpu.VMEM(grid_shape, bf16),
            pltpu.VMEM((modes, D), bf16),
            pltpu.VMEM((2 * NB * BS, BS), bf16),
            pltpu.VMEM((2 * NB * BS, BS), bf16),
            pltpu.VMEM(grid_shape, bf16),
            pltpu.VMEM((FF // 128, LON, row_count, 128), bf16),
            pltpu.VMEM((rank, FF), bf16),
            pltpu.VMEM((2 * NB * BS, 4 * BS), bf16),
            pltpu.VMEM((2 * NB * BS, 4 * BS), bf16),
            pltpu.VMEM((modes, D), bf16),
            pltpu.VMEM((modes, D), f32),
            pltpu.VMEM((modes, D), bf16),
            pltpu.VMEM((modes, D), bf16),
            pltpu.VMEM((modes, D), bf16),
            pltpu.VMEM(slab, bf16),
            pltpu.VMEM(slab, bf16),
            pltpu.VMEM(slab, bf16),
            pltpu.VMEM(slab, bf16),
            pltpu.VMEM((data_count, rank // data_count, D), f32),
            pltpu.VMEM((data_count, rank // data_count, D), f32),
            pltpu.VMEM((rank // data_count, D), f32),
            pltpu.VMEM((space_count, rank // data_count, D), f32),
            pltpu.VMEM((data_count, rank // data_count, D), f32),
            pltpu.VMEM((data_count, space_count, rank, 256), bf16),
            pltpu.VMEM((data_count, space_count, rank, 256), bf16),
            pltpu.VMEM((space_count, rank, 256), bf16),
            pltpu.VMEM((space_count, rank, 256), bf16),
            pltpu.VMEM((2, 2, 2 * BS, 4 * BS), bf16),
            pltpu.VMEM((2, 2 * BS, 4 * BS), bf16),
            pltpu.VMEM((2 * BS, 4 * BS), bf16),
            pltpu.VMEM((space_count, 2 * BS // space_count, 4 * BS), bf16),
            pltpu.VMEM((space_count, 2 * BS // space_count, 4 * BS), bf16),
            pltpu.VMEM((space_count, 2 * BS // space_count, 4 * BS), bf16),
            pltpu.SemaphoreType.DMA((3 * (D // 128) + FF // 128 + 8,)),
            pltpu.SemaphoreType.DMA((copies,)),
            pltpu.SemaphoreType.DMA((copies,)),
        ],
        compiler_params=pltpu.CompilerParams(
            collective_id=0, has_side_effects=True, vmem_limit_bytes=40 * 1024 * 1024
        ),
        name="fused_filter_sketch",
    )(
        grad_mid.transpose(0, 2, 1, 3).reshape(LON, row_count, D),
        spectrum.reshape(modes, D),
        filter_inner.reshape(2 * NB * BS, BS),
        filter_outer.reshape(2 * NB * BS, BS),
        cutoff.reshape(1, KLON),
        normed_mid.transpose(0, 2, 1, 3).reshape(LON, row_count, D),
        hidden_grad.transpose(0, 2, 1, 3).reshape(LON, row_count, FF),
        power_start.T,
        lon_table,
        spread,
        lat_table,
        back_table,
    )
    grid = grid_out.reshape(1, LON, row_count, D).transpose(0, 2, 1, 3)
    return (grid, inner_out, outer_out, left_out.T, right_out.T)


def solution(mesh):
    in_specs = (
        P(("groups", "dp"), "space", None, None),
        P(None, ("groups", "dp"), None, "space", None),
        P(),
        P(),
        P(),
        P(("groups", "dp"), "space", None, None),
        P(("groups", "dp"), "space", None, None),
        P(),
    )
    out_specs = (
        P(("groups", "dp"), "space", None, None),
        P("groups", "dp", None, None),
        P("groups", "dp", None, None),
        P("groups", None),
        P(("groups", "space", "dp"), None),
    )
    fits = mesh.shape["space"] == 4 and mesh.shape["dp"] == 4
    chosen = fused_body if fits else body
    return jax.shard_map(chosen, mesh=mesh, in_specs=in_specs, out_specs=out_specs, check_vma=False)
```
